32 devices in a mesh: dp: 4 (over z), wide: 2 (over y), narrow: 4 (over x, core).
Axes of the slice: x: 2, y: 2, z: 4, core: 2. Of those that a mesh axis runs over, the one named last changes fastest.
Arguments:
- inputs: bfloat16 [16384, 1024], P(('dp', 'wide', 'narrow')), may hold values from -6 to 6
- segments: int32 [16384], P(('dp', 'wide', 'narrow')), may hold values from -1 to 7, as said below
- first_gain: float32 [1024], replicated, may hold values from 0.25 to 1.75
- first_shift: float32 [1024], replicated, may hold values from -1.75 to 1.75
- qkv_weight: bfloat16 [1024, 3, 1024], P('narrow', None, 'wide'), may hold values from -0.1875 to 0.1875
- qv_bias: bfloat16 [2, 1024], P(None, 'wide'), may hold values from -3 to 3
- out_weight: bfloat16 [1024, 1024], P('wide', 'narrow'), may hold values from -0.75 to 0.75
- out_bias: bfloat16 [1024], replicated, may hold values from -3 to 3
- second_gain: float32 [1024], replicated, may hold values from 0.25 to 1.75
- second_shift: float32 [1024], replicated, may hold values from -1.75 to 1.75
- up_weight: bfloat16 [1024, 4096], P('narrow', 'wide'), may hold values from -0.1875 to 0.1875
- up_bias: bfloat16 [4096], P('wide'), may hold values from -3 to 3
- down_weight: bfloat16 [4096, 1024], P('wide', 'narrow'), may hold values from -0.09375 to 0.09375
- down_bias: bfloat16 [1024], replicated, may hold values from -3 to 3
- cotangent: bfloat16 [16384, 1024], P(('dp', 'wide', 'narrow')), may hold values from -6 to 6
Outputs:
- output: bfloat16 [16384, 1024], P(('dp', 'wide', 'narrow'))
- input_grad: bfloat16 [16384, 1024], P(('dp', 'wide', 'narrow'))
- first_gain_grad: float32 [1024], replicated
- first_shift_grad: float32 [1024], replicated
- qkv_grad: float32 [1024, 3, 1024], P('narrow', None, 'wide')
- qv_bias_grad: float32 [2, 1024], P(None, ('wide', 'narrow'))
- out_grad: float32 [1024, 1024], P('wide', 'narrow')
- out_bias_grad: float32 [1024], replicated
- second_gain_grad: float32 [1024], replicated
- second_shift_grad: float32 [1024], replicated
- up_grad: float32 [1024, 4096], P('narrow', 'wide')
- up_bias_grad: float32 [4096], P(('wide', 'narrow'))
- down_grad: float32 [4096, 1024], P('wide', 'narrow')
- down_bias_grad: float32 [1024], replicated
The draws below stay inside these ranges and needn't reach their ends.
Inputs may be any that keep to these rules, and one draw needn't show every extreme that they name: `segments`: each aligned run of 512 rows is one sequence: its rows carry segment numbers 0 to 7 in order, every one of them present on at least one row, followed in some sequences by padding rows numbered -1.
All inputs are finite; a program needn't handle non-finite values.
Results may differ from the reference program's by a relative error of at most 0.02.
Values may be sent and summed in bfloat16 or wider, within the bound.
No kernel may reach another device: no remote copies, remote signals or barrier semaphores. Data moves between devices by JAX's collectives and lax.ppermute only.
A program may use at most 128 MiB of HBM per device.

```python
from functools import partial
import jax
import jax.numpy as jnp
from jax import lax

D = 1024
H = 16
HD = 64
FF = 4096
LEN = 512
SEGS = 8
GROUPS = 2
TOKENS = 16384


def draw_segments(key, part):
    key = jax.random.fold_in(key, 11)
    sequences = TOKENS // LEN
    seq_keys = jax.random.split(key, sequences)

    def one_sequence(seq_key):
        first_key, second_key = jax.random.split(seq_key)
        boundary = jax.random.permutation(first_key, LEN * 3 // 4 - 1)[:SEGS - 1] + 1
        places = jnp.arange(LEN, dtype=jnp.int32)
        numbers = jnp.sum((places[:, None] >= boundary[None, :]).astype(jnp.int32), axis=1)
        padding = jax.random.randint(second_key, (), 0, LEN // 4)
        return jnp.where(places >= LEN - padding, -1, numbers).astype(jnp.int32)
    return jax.vmap(one_sequence)(seq_keys).reshape(TOKENS)


def level_of(own_key, shape, cuts, least, largest):
    def one(dim, shards_of):
        steps = jax.random.uniform(jax.random.fold_in(jax.random.fold_in(own_key, 6), dim), (shards_of,), jnp.float32, least / len(cuts), largest / len(cuts))
        return jnp.repeat(jnp.exp(steps), shape[dim] // shards_of).reshape((-1,) + (1,) * (len(shape) - dim - 1))

    level = one(*cuts[0])
    for cut in cuts[1:]:
        level = level * one(*cut)
    return level


def bell_draw(stream_key, dims, scale, reach, pieces=(), held_as=jnp.bfloat16):
    values = scale * jax.random.normal(stream_key, dims, jnp.float32)
    if pieces:
        values = values * level_of(stream_key, dims, pieces, -0.22, 0.18)
    return jnp.clip(values, -reach, reach).astype(held_as)


def setup_inputs(seed: int = 0) -> dict:
    key_list = jax.random.split(jax.random.key(seed), 16)
    return {
        "inputs": bell_draw(key_list[0], (TOKENS, D), 1.0, 6.0, ((0, 32),)),
        "segments": draw_segments(jax.random.fold_in(key_list[15], 71), 0),
        "first_gain": jnp.clip(1.0 + 0.15 * jax.random.normal(key_list[2], (D,), jnp.float32), 0.25, 1.75),
        "first_shift": bell_draw(key_list[3], (D,), 0.3, 1.75, (), jnp.float32),
        "qkv_weight": bell_draw(key_list[4], (D, 3, D), D ** -0.5, 0.1875, ((0, 4), (2, 2))),
        "qv_bias": bell_draw(key_list[5], (2, D), 0.5, 3.0, ((1, 2),)),
        "out_weight": bell_draw(key_list[6], (D, D), (D // 16) ** -0.5, 0.75, ((0, 2), (1, 4))),
        "out_bias": bell_draw(key_list[7], (D,), 0.5, 3.0),
        "second_gain": jnp.clip(1.0 + 0.15 * jax.random.normal(key_list[8], (D,), jnp.float32), 0.25, 1.75),
        "second_shift": bell_draw(key_list[9], (D,), 0.3, 1.75, (), jnp.float32),
        "up_weight": bell_draw(key_list[10], (D, FF), D ** -0.5, 0.1875, ((0, 4), (1, 2))),
        "up_bias": bell_draw(key_list[11], (FF,), 0.5, 3.0, ((0, 2),)),
        "down_weight": bell_draw(key_list[12], (FF, D), FF ** -0.5, 0.09375, ((0, 2), (1, 4))),
        "down_bias": bell_draw(key_list[13], (D,), 0.5, 3.0),
        "cotangent": bell_draw(key_list[14], (TOKENS, D), 1.0, 6.0, ((0, 32),)),
    }


EPSILON = 1e-06
MASKED = -1e+30
SQRT_HALF = 0.7071067811865476
HIGHEST = lax.Precision.HIGHEST

@jax.custom_vjp
def low(v):
    return lax.optimization_barrier(v.astype(jnp.bfloat16)).astype(jnp.float32)

@jax.custom_vjp
def low_back(v):
    return v

def low_keep(v):
    return (low(v), None)

def low_pass(kept, grad):
    return (grad,)

def back_keep(v):
    return (v, None)

def back_low(kept, grad):
    return (low(grad),)
low.defvjp(low_keep, low_pass)
low_back.defvjp(back_keep, back_low)

def layer_norm(values, gain, shift):
    average = lax.optimization_barrier(jnp.mean(values, axis=-1, keepdims=True))
    centred = values - average
    variance = lax.optimization_barrier(jnp.mean(centred * centred, axis=-1, keepdims=True))
    return centred * lax.rsqrt(variance + EPSILON) * gain + shift

def gaussian_unit(values):
    return 0.5 * values * (1.0 + lax.erf(values * SQRT_HALF))

def block_forward(params, inputs, segments):
    first_gain, first_shift, qkv_weight, qv_bias, out_weight, out_bias, second_gain, second_shift, up_weight, up_bias, down_weight, down_bias = params
    row_count = inputs.shape[0]
    part_width = D // GROUPS
    heads_local = H // GROUPS
    hidden_width = FF // GROUPS
    sequences = row_count // LEN
    keep_rows = (segments >= 0).astype(jnp.float32)[:, None]
    normed_one = low(layer_norm(inputs, first_gain, first_shift))
    spread_one = low_back(jnp.broadcast_to(normed_one, (GROUPS, row_count, D)))
    qkv_groups = qkv_weight.reshape(D, 3, GROUPS, part_width).transpose(2, 0, 1, 3).reshape(GROUPS, D, 3 * part_width)
    projected = jnp.einsum('gtd,gdc->gtc', spread_one, qkv_groups, precision=HIGHEST).reshape(GROUPS, row_count, 3, part_width)
    bias_rows = jnp.stack([qv_bias[0], jnp.zeros((D,), jnp.float32), qv_bias[1]])
    bias_groups = bias_rows.reshape(3, GROUPS, part_width).transpose(1, 0, 2)
    projected = low(low_back(projected + bias_groups[:, None, :, :]))
    shaped = projected.reshape(GROUPS, sequences, LEN, 3, heads_local, HD)
    query_rows = shaped[:, :, :, 0]
    key_rows = shaped[:, :, :, 1]
    value_rows = shaped[:, :, :, 2]
    raw_scores = jnp.einsum('gsqhe,gskhe->gshqk', query_rows, key_rows, precision=HIGHEST)
    labels = segments.reshape(sequences, LEN)
    allowed = (labels[:, :, None] == labels[:, None, :])[None, :, None]
    scores = low_back(raw_scores * HD ** (-0.5))
    scores = jnp.where(allowed, scores, MASKED)
    highest = lax.optimization_barrier(jnp.max(scores, axis=-1, keepdims=True))
    weights = jnp.exp(scores - highest)
    softmax_out = low(weights / lax.optimization_barrier(jnp.sum(weights, axis=-1, keepdims=True)))
    attended = jnp.einsum('gshqk,gskhe->gsqhe', softmax_out, value_rows, precision=HIGHEST)
    attended = low(low_back(attended.reshape(GROUPS, row_count, part_width)))
    out_groups = out_weight.reshape(GROUPS, part_width, D)
    partial_one = low(jnp.einsum('gtc,gcd->gtd', attended, out_groups, precision=HIGHEST))
    middle = inputs + low_back(lax.optimization_barrier(jnp.sum(partial_one, axis=0))) + out_bias
    normed_two = low(layer_norm(middle, second_gain, second_shift))
    spread_two = low_back(jnp.broadcast_to(normed_two, (GROUPS, row_count, D)))
    up_groups = up_weight.reshape(D, GROUPS, hidden_width).transpose(1, 0, 2)
    before = jnp.einsum('gtd,gdf->gtf', spread_two, up_groups, precision=HIGHEST) + up_bias.reshape(GROUPS, 1, hidden_width)
    hidden = low(gaussian_unit(low_back(before)))
    down_groups = down_weight.reshape(GROUPS, hidden_width, D)
    partial_two = low(jnp.einsum('gtf,gfd->gtd', hidden, down_groups, precision=HIGHEST))
    return keep_rows * (middle + low_back(lax.optimization_barrier(jnp.sum(partial_two, axis=0))) + down_bias)

def reference(inputs, segments, first_gain, first_shift, qkv_weight, qv_bias, out_weight, out_bias, second_gain, second_shift, up_weight, up_bias, down_weight, down_bias, cotangent):
    params = tuple((array.astype(jnp.float32) for array in (first_gain, first_shift, qkv_weight, qv_bias, out_weight, out_bias, second_gain, second_shift, up_weight, up_bias, down_weight, down_bias)))
    group_rows = 4 * LEN
    blocks = TOKENS // group_rows

    def one_block(totals, position):
        offset = position * group_rows
        block_in = lax.dynamic_slice_in_dim(inputs, offset, group_rows, 0).astype(jnp.float32)
        block_labels = lax.dynamic_slice_in_dim(segments, offset, group_rows, 0)
        block_cot = lax.dynamic_slice_in_dim(cotangent, offset, group_rows, 0).astype(jnp.float32)
        result, pullback = jax.vjp(partial(block_forward, segments=block_labels), params, block_in)
        grad_params, grad_in = pullback(block_cot)
        totals = jax.tree.map(jnp.add, totals, grad_params)
        return (totals, (result.astype(jnp.bfloat16), grad_in.astype(jnp.bfloat16)))
    start_totals = jax.tree.map(jnp.zeros_like, params)
    totals, (outputs, input_grads) = lax.scan(one_block, start_totals, jnp.arange(blocks, dtype=jnp.int32))
    return (outputs.reshape(TOKENS, D), input_grads.reshape(TOKENS, D), totals[0], totals[1], totals[2], totals[3], totals[4], totals[5], totals[6], totals[7], totals[8], totals[9], totals[10], totals[11])
```

```python
from functools import partial

import jax
import jax.numpy as jnp
import numpy as np
from jax import lax
from jax.experimental import pallas as pl
from jax.experimental.pallas import tpu as pltpu
from jax.sharding import PartitionSpec as P

HD = 64
LEN = 512
LANES = 128
EPSILON = 1e-06
MASKED = -1e30
SQRT_HALF = 0.7071067811865476
DENSITY_SCALE = 0.3989422804014327
BF = jnp.bfloat16
F32 = jnp.float32
MIB = 1 << 20

NN = (((1,), (0,)), ((), ()))
NT = (((1,), (1,)), ((), ()))


def dot(left, right, dims=NN):
    return lax.dot_general(left, right, dims, preferred_element_type=F32)


def call(body, grid, ins, outs, operands, scratch=(), flops=0, name=None, vmem=58, tables=0):
    moved = sum(int(np.prod(o.shape)) * o.dtype.itemsize for o in operands)
    moved += sum(int(np.prod(o.shape)) * o.dtype.itemsize for _, o in outs)
    return pl.pallas_call(
        body,
        out_shape=[o for _, o in outs],
        grid_spec=pltpu.PrefetchScalarGridSpec(
            num_scalar_prefetch=tables,
            grid=grid,
            in_specs=ins,
            out_specs=[s for s, _ in outs],
            scratch_shapes=list(scratch),
        ),
        compiler_params=pltpu.CompilerParams(vmem_limit_bytes=vmem * MIB),
        cost_estimate=pl.CostEstimate(flops=int(flops), bytes_accessed=moved, transcendentals=0),
        name=name,
    )(*operands)


def after(value, *others):
    return lax.optimization_barrier((value, *others))[0]


def shape(dims, dtype):
    return jax.ShapeDtypeStruct(dims, dtype)


def columns(meta, ref, places, width):
    return jnp.concatenate(
        [ref[:, pl.ds(pl.multiple_of(meta[r], width), width)] for r in range(places)], axis=1
    )


def norm_stats(values):
    average = jnp.mean(values, axis=-1, keepdims=True)
    centred = values - average
    variance = jnp.mean(centred * centred, axis=-1, keepdims=True)
    scaled = lax.rsqrt(variance + EPSILON)
    return centred * scaled, scaled


def norm_back(upstream, gain, normal, scaled):
    inner = upstream * gain
    first_term = jnp.mean(inner, axis=-1, keepdims=True)
    second_term = jnp.mean(inner * normal, axis=-1, keepdims=True)
    return scaled * (inner - first_term - normal * second_term)


def first_norm(inputs, cotangent, keep, gain, shift, meta, places):
    rows, width = inputs.shape
    block = 128
    part = width // places

    def body(meta, x, cot, keep, gain, shift, normed, normed_t, low, low_t):
        normal, _ = norm_stats(columns(meta, x, places, part).astype(F32))
        out = normal * columns(meta, gain, places, part) + columns(meta, shift, places, part)
        normed[...] = out.astype(BF)
        normed_t[...] = out.T.astype(BF)
        grad = columns(meta, cot, places, part).astype(F32) * keep[...]
        low[...] = grad.astype(BF)
        low_t[...] = grad.T.astype(BF)

    tall = pl.BlockSpec((block, width), lambda i, *_: (i, 0))
    wide = pl.BlockSpec((width, block), lambda i, *_: (0, i))
    vector = pl.BlockSpec((1, width), lambda i, *_: (0, 0))
    mark = pl.BlockSpec((block, 1), lambda i, *_: (i, 0))
    return call(
        body,
        (rows // block,),
        [tall, tall, mark, vector, vector],
        [
            (tall, shape((rows, width), BF)),
            (wide, shape((width, rows), BF)),
            (tall, shape((rows, width), BF)),
            (wide, shape((width, rows), BF)),
        ],
        (meta, inputs, cotangent, keep, gain, shift),
        tables=1,
        name="first_norm",
    )


def tile_of(refs, step, steps):
    blocks = []
    for parts in refs:
        value = parts[0][...]
        for k in range(1, len(parts)):
            value = jnp.where(step >= k * (steps // len(parts)), parts[k][...], value)
        blocks.append(value)
    return jnp.concatenate(blocks, axis=0)


def tile_specs(pieces, width, steps):
    specs, operands, counts = [], [], []
    for parts in pieces:
        counts.append(len(parts))
        per = steps // len(parts)
        for k, array in enumerate(parts):
            specs.append(
                pl.BlockSpec(
                    (array.shape[0], width),
                    lambda j, *_, k=k, per=per: (0, jnp.clip(j - k * per, 0, per - 1)),
                )
            )
            operands.append(array)
    return specs, operands, counts


def regroup(refs, counts):
    grouped, at = [], 0
    for count in counts:
        grouped.append(refs[at : at + count])
        at += count
    return grouped


def attend(normed, pieces, bias, labels_col, labels_row, halves):
    rows, width = normed.shape
    total = sum(p.shape[1] for p in pieces[0])
    wide = total // halves
    part = wide // 4
    heads = part // HD
    specs, weights, counts = tile_specs(pieces, wide, halves)

    def body(normed, *refs):
        weight_refs = regroup(refs[: len(weights)], counts)
        bias, lc, lr, qkv, attended, probs, inverses, branch, mask = refs[len(weights) :]
        step = pl.program_id(0)

        @pl.when(step == 0)
        def _():
            mask[...] = jnp.where(lc[...] == lr[...], 0.0, MASKED)

        tile = tile_of(weight_refs, step, halves)
        projected = dot(normed[...], tile[:, : 3 * part]) + bias[...].astype(F32)
        low = projected.astype(BF)
        qkv[...] = low
        lane = lax.broadcasted_iota(jnp.int32, (1, LANES), 1)
        per = LANES // HD
        queries, keys, values = [], [], []
        for pair in range(part // LANES):
            at = pair * LANES
            queries.append(low[:, at : at + LANES] * jnp.asarray(HD**-0.5, BF))
            keys.append(low[:, part + at : part + at + LANES])
            values.append(low[:, 2 * part + at : 2 * part + at + LANES].T)

        def scores_of(head):
            pair, e = divmod(head, per)
            mine = (lane >= e * HD) & (lane < (e + 1) * HD)
            key = jnp.where(mine, keys[pair], jnp.zeros_like(keys[pair]))
            return dot(key, queries[pair], NT)

        coming, outs = scores_of(0), []
        for head in range(heads):
            scores = coming
            if head + 1 < heads:
                coming = scores_of(head + 1)
            pair, e = divmod(head, per)
            scores = scores + mask[...]
            weight = jnp.exp(scores - jnp.max(scores, axis=0, keepdims=True))
            inverse = 1.0 / jnp.sum(weight, axis=0, keepdims=True)
            prob = weight.astype(BF)
            probs[head] = prob
            inverses[0, head : head + 1, :] = inverse
            outs.append(dot(values[pair][e * HD : (e + 1) * HD], prob) * inverse)
            if e == per - 1:
                at = pair * LANES
                attended[:, at : at + LANES] = jnp.concatenate(outs, axis=0).T.astype(BF)
                outs = []
        product = dot(attended[...], tile[:, 3 * part :], NT)

        @pl.when(step == 0)
        def _():
            branch[...] = product

        @pl.when(step > 0)
        def _():
            branch[...] += product

    fixed = lambda *dims: pl.BlockSpec(dims, lambda j, *_: (0,) * len(dims))
    return call(
        body,
        (halves,),
        [fixed(rows, width)]
        + specs
        + [pl.BlockSpec((1, 3 * part), lambda j: (0, j)), fixed(rows, 1), fixed(1, rows)],
        [
            (pl.BlockSpec((rows, 3 * part), lambda j: (0, j)), shape((rows, halves * 3 * part), BF)),
            (pl.BlockSpec((rows, part), lambda j: (0, j)), shape((rows, halves * part), BF)),
            (
                pl.BlockSpec((heads, rows, rows), lambda j: (j, 0, 0)),
                shape((halves * heads, rows, rows), BF),
            ),
            (pl.BlockSpec((1, heads, rows), lambda j: (j, 0, 0)), shape((halves, heads, rows), F32)),
            (fixed(rows, width), shape((rows, width), F32)),
        ],
        (normed, *weights, bias, labels_col, labels_row),
        scratch=[pltpu.VMEM((rows, rows), F32)],
        flops=2 * rows * width * total + halves * heads * 8 * rows * rows * HD,
        name="attend",
    )


def second_norm(inputs, branches, out_bias, gain, shift, meta, places):
    rows, width = inputs.shape
    block = 128
    part = width // places
    count = len(branches)

    def body(meta, x, *refs):
        bias, gain, shift, middle, normed, normed_t = refs[count:]
        value = columns(meta, x, places, part).astype(F32)
        total = refs[0][...]
        for ref in refs[1:count]:
            total = total + ref[...]
        value = value + total + columns(meta, bias, places, part)
        middle[...] = value
        normal, _ = norm_stats(value)
        out = normal * columns(meta, gain, places, part) + columns(meta, shift, places, part)
        normed[...] = out.astype(BF)
        normed_t[...] = out.T.astype(BF)

    tall = pl.BlockSpec((block, width), lambda i, *_: (i, 0))
    wide = pl.BlockSpec((width, block), lambda i, *_: (0, i))
    vector = pl.BlockSpec((1, width), lambda i, *_: (0, 0))
    return call(
        body,
        (rows // block,),
        [tall] * (1 + count) + [vector] * 3,
        [
            (tall, shape((rows, width), F32)),
            (tall, shape((rows, width), BF)),
            (wide, shape((width, rows), BF)),
        ],
        (meta, inputs, *branches, out_bias, gain, shift),
        tables=1,
        name="second_norm",
    )


def up_steps(total, halves):
    return max(halves, total // 512)


def up(normed, pieces, bias, halves):
    rows, width = normed.shape
    total = sum(p.shape[1] for p in pieces[0])
    steps = up_steps(total, halves)
    wide = total // steps
    specs, weights, counts = tile_specs(pieces, wide, steps)

    def body(normed, *refs):
        weight_refs = regroup(refs[: len(weights)], counts)
        bias, hidden, slope = refs[len(weights) :]
        tile = tile_of(weight_refs, pl.program_id(0), steps)
        before = dot(normed[...], tile) + bias[...].astype(F32)
        below = 0.5 * (1.0 + lax.erf(before * SQRT_HALF))
        hidden[...] = (before * below).astype(BF)
        density = jnp.exp(before * before * -0.5) * DENSITY_SCALE
        slope[...] = (below + before * density).astype(BF)

    tall = pl.BlockSpec((rows, wide), lambda j: (0, j))
    return call(
        body,
        (steps,),
        [pl.BlockSpec((rows, width), lambda j: (0, 0))]
        + specs
        + [pl.BlockSpec((1, wide), lambda j: (0, j))],
        [(tall, shape((rows, total), BF)), (tall, shape((rows, total), BF))],
        (normed, *weights, bias),
        flops=2 * rows * width * total,
        name="up",
    )


def mlp_back(low, hidden, slope, up_pieces, down_pieces, halves):
    rows, width = low.shape
    total = hidden.shape[1]
    steps = up_steps(total, halves)
    wide = total // steps
    up_specs, up_weights, up_counts = tile_specs(up_pieces, wide, steps)
    down_specs, down_weights, down_counts = tile_specs(down_pieces, wide, steps)
    count = len(up_weights)

    def body(low, hidden, slope, *refs):
        up_refs = regroup(refs[:count], up_counts)
        down_refs = regroup(refs[count : 2 * count], down_counts)
        before, sums, mlp, normed = refs[2 * count :]
        step = pl.program_id(0)
        down_tile = tile_of(down_refs, step, steps)
        up_tile = tile_of(up_refs, step, steps)
        grad = dot(low[...], down_tile) * slope[...].astype(F32)
        grad_low = grad.astype(BF)
        before[...] = grad_low
        sums[...] = jnp.sum(grad_low.astype(F32), axis=0, keepdims=True)
        product = dot(hidden[...], down_tile, NT)
        back = dot(grad_low, up_tile, NT)

        @pl.when(step == 0)
        def _():
            mlp[...] = product
            normed[...] = back

        @pl.when(step > 0)
        def _():
            mlp[...] += product
            normed[...] += back

    fixed = pl.BlockSpec((rows, width), lambda j: (0, 0))
    tall = pl.BlockSpec((rows, wide), lambda j: (0, j))
    return call(
        body,
        (steps,),
        [fixed, tall, tall] + up_specs + down_specs,
        [
            (tall, shape((rows, total), BF)),
            (pl.BlockSpec((1, wide), lambda j: (0, j)), shape((1, total), F32)),
            (fixed, shape((rows, width), F32)),
            (fixed, shape((rows, width), F32)),
        ],
        (low, hidden, slope, *up_weights, *down_weights),
        flops=6 * rows * width * total,
        name="mlp_back",
    )


def second_norm_back(middle, backs, low, gain, meta, places):
    rows, width = middle.shape
    block = 128
    part = width // places
    count = len(backs)

    def body(meta, middle, low, *refs):
        gain, grad, grad_low, grad_t, sums = refs[count:]
        upstream = refs[0][...]
        for ref in refs[1:count]:
            upstream = upstream + ref[...]
        normal, scaled = norm_stats(middle[...])
        out = low[...].astype(F32)
        total = out + norm_back(upstream, columns(meta, gain, places, part), normal, scaled)
        grad[...] = total
        grad_low[...] = total.astype(BF)
        grad_t[...] = total.T.astype(BF)

        @pl.when(pl.program_id(0) == 0)
        def _():
            sums[...] = jnp.zeros_like(sums)

        for k, value in enumerate((upstream * normal, upstream, total, out)):
            added = jnp.sum(value, axis=0, keepdims=True)
            for r in range(places):
                spot = pl.ds(pl.multiple_of(meta[r], part), part)
                sums[k : k + 1, spot] += added[:, r * part : (r + 1) * part]

    tall = pl.BlockSpec((block, width), lambda i, *_: (i, 0))
    wide = pl.BlockSpec((width, block), lambda i, *_: (0, i))
    vector = pl.BlockSpec((1, width), lambda i, *_: (0, 0))
    return call(
        body,
        (rows // block,),
        [tall, tall] + [tall] * count + [vector],
        [
            (tall, shape((rows, width), F32)),
            (tall, shape((rows, width), BF)),
            (wide, shape((width, rows), BF)),
            (pl.BlockSpec((4, width), lambda i, *_: (0, 0)), shape((4, width), F32)),
        ],
        (meta, middle, low, *backs, gain),
        tables=1,
        name="second_norm_back",
    )


def attend_back(grad_low, pieces, qkv, probs, inverses, halves):
    rows, width = grad_low.shape
    total = sum(p.shape[1] for p in pieces[0])
    wide = total // halves
    part = wide // 4
    heads = part // HD
    specs, weights, counts = tile_specs(pieces, wide, halves)

    def body(grad_low, *refs):
        weight_refs = regroup(refs[: len(weights)], counts)
        qkv, probs, inverses, grads, sums, back = refs[len(weights) :]
        step = pl.program_id(0)
        tile = tile_of(weight_refs, step, halves)
        upstream = dot(grad_low[...], tile[:, 3 * part :]).astype(BF)
        lane = lax.broadcasted_iota(jnp.int32, (1, LANES), 1)
        factor = HD**-0.5
        per = LANES // HD
        queries, keys, values, ups = [], [], [], []
        for pair in range(part // LANES):
            at = pair * LANES
            queries.append(qkv[:, at : at + LANES] * jnp.asarray(factor, BF))
            key = qkv[:, part + at : part + at + LANES]
            keys.append((key * jnp.asarray(factor, BF)).T)
            values.append(qkv[:, 2 * part + at : 2 * part + at + LANES])
            up_t = upstream[:, at : at + LANES].T.astype(F32)
            scaled = [
                up_t[e * HD : (e + 1) * HD] * inverses[0, pair * per + e : pair * per + e + 1, :]
                for e in range(per)
            ]
            ups.append(jnp.concatenate(scaled, axis=0).T.astype(BF))

        def own(value, e):
            mine = (lane >= e * HD) & (lane < (e + 1) * HD)
            return jnp.where(mine, value, jnp.zeros_like(value))

        def first_of(head):
            pair, e = divmod(head, per)
            return dot(own(values[pair], e), ups[pair], NT)

        coming = first_of(0)
        for head in range(heads):
            pair, e = divmod(head, per)
            at = pair * LANES
            grad_probs = coming
            if head + 1 < heads:
                coming = first_of(head + 1)
            prob = probs[head].astype(F32)
            delta = jnp.sum(prob * grad_probs, axis=0, keepdims=True)
            delta = delta * inverses[0, head : head + 1, :]
            made = (prob * (grad_probs - delta)).astype(BF)
            if e == 0:
                grad_key = dot(made, own(queries[pair], e))
                grad_value = dot(probs[head], own(ups[pair], e))
                query_t = []
            else:
                grad_key = grad_key + dot(made, own(queries[pair], e))
                grad_value = grad_value + dot(probs[head], own(ups[pair], e))
            query_t.append(dot(keys[pair][e * HD : (e + 1) * HD], made))
            if e == per - 1:
                grad_query = jnp.concatenate(query_t, axis=0).T
                for c, grad in enumerate((grad_query, grad_key, grad_value)):
                    grads[:, c * part + at : c * part + at + LANES] = grad.astype(BF)
        made = grads[...]
        sums[...] = jnp.sum(made.astype(F32), axis=0, keepdims=True)
        product = dot(made, tile[:, : 3 * part], NT)

        @pl.when(step == 0)
        def _():
            back[...] = product

        @pl.when(step > 0)
        def _():
            back[...] += product

    fixed = pl.BlockSpec((rows, width), lambda j: (0, 0))
    wide_rows = pl.BlockSpec((rows, 3 * part), lambda j: (0, j))
    return call(
        body,
        (halves,),
        [fixed]
        + specs
        + [
            wide_rows,
            pl.BlockSpec((heads, rows, rows), lambda j: (j, 0, 0)),
            pl.BlockSpec((1, heads, rows), lambda j: (j, 0, 0)),
        ],
        [
            (wide_rows, shape((rows, halves * 3 * part), BF)),
            (pl.BlockSpec((1, 3 * part), lambda j: (0, j)), shape((1, halves * 3 * part), F32)),
            (fixed, shape((rows, width), F32)),
        ],
        (grad_low, *weights, qkv, probs, inverses),
        flops=2 * rows * width * total + halves * heads * 8 * rows * rows * HD,
        name="attend_back",
    )


def finish(inputs, middle, mlps, grad_middle, backs, keep, gain, down_bias, meta, places):
    rows, width = inputs.shape
    block = 128
    part = width // places
    count = len(mlps)

    def body(meta, x, middle, grad, keep, *refs):
        gain, bias, output, input_grad, sums = refs[2 * count :]
        mlp, upstream = refs[0][...], refs[count][...]
        for k in range(1, count):
            mlp = mlp + refs[k][...]
            upstream = upstream + refs[count + k][...]
        out = (middle[...] + mlp + columns(meta, bias, places, part)) * keep[...]
        normal, scaled = norm_stats(columns(meta, x, places, part).astype(F32))
        back = grad[...] + norm_back(upstream, columns(meta, gain, places, part), normal, scaled)

        @pl.when(pl.program_id(0) == 0)
        def _():
            sums[...] = jnp.zeros_like(sums)

        gains = jnp.sum(upstream * normal, axis=0, keepdims=True)
        shifts = jnp.sum(upstream, axis=0, keepdims=True)
        for r in range(places):
            spot = pl.ds(pl.multiple_of(meta[r], part), part)
            here = slice(r * part, (r + 1) * part)
            output[:, spot] = out[:, here].astype(BF)
            input_grad[:, spot] = back[:, here].astype(BF)
            sums[0:1, spot] += gains[:, here]
            sums[1:2, spot] += shifts[:, here]

    tall = pl.BlockSpec((block, width), lambda i, *_: (i, 0))
    vector = pl.BlockSpec((1, width), lambda i, *_: (0, 0))
    mark = pl.BlockSpec((block, 1), lambda i, *_: (i, 0))
    return call(
        body,
        (rows // block,),
        [tall, tall, tall, mark] + [tall] * (2 * count) + [vector, vector],
        [
            (tall, shape((rows, width), BF)),
            (tall, shape((rows, width), BF)),
            (pl.BlockSpec((2, width), lambda i, *_: (0, 0)), shape((2, width), F32)),
        ],
        (meta, inputs, middle, grad_middle, keep, *mlps, *backs, gain, down_bias),
        tables=1,
        name="finish",
    )


def bundle_plan(groups, halves):
    plan = {"x": [(1, 0, 0)] + [(1, y, 0) for y in range(1, groups)]}
    for y in range(1, groups):
        if halves > 1:
            plan["y", y] = [(0, y, 1), (1, y, 1)]
        plan["keep", y] = [(0, y, 0)]
    if halves > 1:
        plan["far"] = [(1, 0, 1)]
    plan["own"] = [(0, 0, h) for h in range(halves)]
    return plan


def weight_grads(plan, lefts, rights, groups, halves):
    width, rows = lefts[0].shape
    part = width // 4
    lines = len(rights)
    blocks = groups * halves // lines
    spans = [array.shape[1] // blocks for array in rights[0]]
    wide = sum(spans)
    kinds = len(spans)
    order = [(y, 0) for y in range(groups)] + [(y, h) for h in range(1, halves) for y in [*range(1, groups), 0]]
    names = list(plan)
    outs, joint = [], {}
    for _ in range(2):
        for name in names:
            steps = [order.index(block[1:]) for block in plan[name]]
            joint[name] = len(set(steps)) == 1
            size = wide * (len(steps) if joint[name] else 1)
            starts = [] if joint[name] else steps[1:]

            def index(i, starts=starts):
                at = 0
                for start in starts:
                    at = at + (i >= start).astype(jnp.int32)
                return (0, at)

            outs.append((pl.BlockSpec((part, size), index), shape((part, wide * len(steps)), BF)))

    def body(*refs):
        left_refs = refs[:kinds]
        right_refs = [refs[kinds + g * kinds : kinds + (g + 1) * kinds] for g in range(lines)]
        out_refs = refs[kinds + lines * kinds :]
        step = pl.program_id(0)
        for s, (y, h) in enumerate(order):

            @pl.when(step == s)
            def _(y=y, h=h):
                line = (y * halves + h) // blocks
                for r in range(4):
                    x, core = divmod(r, 2)
                    here = slice(r * part, (r + 1) * part)
                    products = [
                        dot(left_refs[k][here, :], right_refs[line][k][...]).astype(BF)
                        for k in range(kinds)
                    ]
                    value = jnp.concatenate(products, axis=1) if kinds > 1 else products[0]
                    for n, name in enumerate(names):
                        if (x, y, h) in plan[name]:
                            at = plan[name].index((x, y, h)) * wide if joint[name] else 0
                            out_refs[core * len(names) + n][:, at : at + wide] = value

    def right_map(g):
        flat = [y * halves + h for y, h in order]
        mine = [(s, at % blocks) for s, at in enumerate(flat) if at // blocks == g]
        def index(i):
            at = mine[0][1]
            for (s0, h0), (s1, h1) in zip(mine, mine[1:]):
                at = at + jnp.where(i > s0, h1 - h0, 0)
            return (0, at)
        return index
    ins = [pl.BlockSpec((width, rows), lambda i: (0, 0)) for _ in lefts]
    operands = list(lefts)
    for g in range(lines):
        for k in range(kinds):
            ins.append(pl.BlockSpec((rows, spans[k]), right_map(g)))
            operands.append(rights[g][k])
    made = call(body, (len(order),), ins, outs, operands, flops=2 * rows * width * wide * len(order), name="weight_grads")
    return dict(zip(names, made[: len(names)])), dict(zip(names, made[len(names) :]))


def shards(
    inputs,
    segments,
    first_gain,
    first_shift,
    qkv_weight,
    qv_bias,
    out_weight,
    out_bias,
    second_gain,
    second_shift,
    up_weight,
    up_bias,
    down_weight,
    down_bias,
    cotangent,
):
    groups = lax.axis_size("wide")
    copies = lax.axis_size("dp")
    places = lax.axis_size("narrow")
    place = lax.axis_index("narrow")
    member = lax.axis_index("wide")
    rows, width = inputs.shape
    part_width = qkv_weight.shape[2]
    hidden_width = up_weight.shape[1]
    part = width // places
    halves = 2 if part_width >= 2 * LANES else 1
    head_part = part_width // halves
    lines = min(2, groups)
    per_line = groups // lines
    steps = per_line * halves

    def members(line):
        return range(line * per_line, (line + 1) * per_line)

    def swap(axis, mask):
        size = lax.axis_size(axis)
        pairs = [(i, i ^ mask) for i in range(size)]
        return lambda value: lax.ppermute(value, axis, pairs)

    core = swap("narrow", 1)
    over_x = swap("narrow", 2)
    over_y = [None] + [swap("wide", m) for m in range(1, groups)]

    meta = jnp.bitwise_xor(place, jnp.arange(places, dtype=jnp.int32)) * part
    row_of = lambda vector: vector.astype(F32).reshape(1, -1)
    keep = (segments >= 0).astype(F32).reshape(rows, 1)
    labels_col = segments.reshape(rows, 1)
    labels_row = segments.reshape(1, rows)

    three = qkv_weight.reshape(part, 3, halves, head_part)
    out_t = out_weight.T.reshape(part, 1, halves, head_part)
    packed = jnp.concatenate([three, out_t], axis=1).transpose(0, 2, 1, 3)
    packed = packed.reshape(part, 4 * part_width)
    small = jnp.concatenate([qv_bias.reshape(-1), up_bias]).reshape(1, -1)
    down_t = down_weight.T

    def split(array):
        wide = array.shape[1] // halves
        return [array[:, h * wide : (h + 1) * wide] for h in range(halves)]

    def reach(own, *others):
        ready = after(own, *others) if others else own
        near = {(0, 0): [own], (1, 0): [over_x(ready)]}
        for y in range(1, groups):
            near[0, y] = [over_y[y](ready)]
        return near

    def forward_far(near):
        made = {}
        for y in range(1, groups):
            made[1, y] = [over_x(split(near[0, y][0])[0])]
            if halves > 1:
                made[1, y].append(over_y[y](split(near[1, 0][0])[1]))
        return made

    def line_of(near, line):
        made = []
        for x in range(2):
            parts = [array for y in members(line) for array in near[x, y]]
            made.append(parts)
            made.append([core(array) for array in parts])
        return made

    small_all = [small] + [over_y[y](small) for y in range(1, groups)]

    turn = []

    def ordered(value, *others):
        return after(value, *turn, *others) if turn or others else value

    def done(made, key):
        turn[:] = [made[key]]
        return made

    def first_stage(near):
        return [near[1, 0][0]] + [near[0, y][0] for y in range(1, groups)]

    def held(near, *others):
        return {
            key: value if key == (0, 0) else [after(array, *others) for array in value]
            for key, value in near.items()
        }

    attn_near = reach(packed)
    normed_one, normed_one_t, low, low_t = done(
        first_norm(
            inputs, cotangent, keep, row_of(first_gain), row_of(first_shift), meta, places
        ),
        0,
    )
    attn_near = held(attn_near, *turn)
    up_near = reach(up_weight, *first_stage(attn_near))

    def qkv_bias(values):
        query = values[:, :part_width].reshape(halves, 1, head_part)
        value = values[:, part_width : 2 * part_width].reshape(halves, 1, head_part)
        return jnp.concatenate([query, jnp.zeros_like(query), value], axis=1).reshape(1, -1)

    forward = []
    far = forward_far(attn_near)
    attn_pieces = [line_of(attn_near | {key: far[key] for key in far if key[1] < per_line}, 0)]
    for line in range(lines):
        if line:
            attn_near = held(attn_near | far, *turn)
            attn_pieces.append(line_of(attn_near, line))
        bias = jnp.concatenate([qkv_bias(small_all[y]) for y in members(line)], axis=1)
        forward.append(
            done(
                attend(
                    ordered(normed_one), attn_pieces[line], bias, labels_col, labels_row, steps
                ),
                1,
            )
        )
    up_near = held(up_near, *turn)
    down_near = reach(down_t, *first_stage(up_near))
    up_near.update(forward_far(up_near))
    up_pieces = [line_of(up_near, line) for line in range(lines)]
    middle, normed_two, normed_two_t = done(
        second_norm(
            ordered(inputs),
            [f[4] for f in forward],
            row_of(out_bias),
            row_of(second_gain),
            row_of(second_shift),
            meta,
            places,
        ),
        0,
    )
    units = []
    for line in range(lines):
        bias = [small_all[y][:, 2 * part_width :] for y in members(line)]
        bias = jnp.concatenate(bias, axis=1)
        units.append(done(up(ordered(normed_two), up_pieces[line], bias, steps), 0))

    plan = bundle_plan(groups, halves)
    block_width = 4 * head_part

    def grads_of(lefts, rights):
        lefts = [ordered(lefts[0])] + lefts[1:]
        mine, other = weight_grads(plan, lefts, rights, groups, halves)
        turn[:] = [mine["own"]]
        return mine, {name: core(value) for name, value in other.items()}

    def both(pair, name):
        return pair[0][name].astype(F32) + pair[1][name].astype(F32)

    def cut(array, k):
        return array[:, k * block_width : (k + 1) * block_width].astype(F32)

    def send_first(pair):
        for_x = both(pair, "x").astype(BF)
        for_y = {}
        if halves > 1:
            for_y = {y: both(pair, ("y", y)).astype(BF) for y in range(1, groups)}
        from_x = over_x(for_x)
        from_y = {y: over_y[y](value) for y, value in for_y.items()}
        turn.extend([for_x, *for_y.values()])
        return from_x, from_y

    def send_second(pair, got):
        from_x = ordered(got[0])
        from_y = {y: ordered(value) for y, value in got[1].items()}
        far = None
        if halves > 1:
            far = both(pair, "far")
            for y in range(1, groups):
                far = far + cut(from_y[y], 1)
            far = far.astype(BF)
        near = [(both(pair, ("keep", y)) + cut(from_x, y)).astype(BF) for y in range(1, groups)]
        late = [over_y[y](near[y - 1]) for y in range(1, groups)]
        far_late = over_x(far) if halves > 1 else None
        turn.extend(near + ([far] if halves > 1 else []))
        return from_x, from_y, late, far_late

    copy_index = lax.axis_index("dp")
    masks = [1 << k for k in range(copies.bit_length() - 1)]
    bits = [(copy_index // mask) % 2 for mask in masks]

    def total_of(pair, got):
        from_x, from_y, late, far_late = got
        late = [ordered(value) for value in late]
        own = both(pair, "own")
        totals = [own[:, h * block_width : (h + 1) * block_width] for h in range(halves)]
        totals[0] = totals[0] + cut(from_x, 0)
        for y in range(1, groups):
            totals[0] = totals[0] + late[y - 1].astype(F32)
            if halves > 1:
                totals[1] = totals[1] + cut(from_y[y], 0)
        if halves > 1:
            totals[1] = totals[1] + ordered(far_late).astype(F32)
        else:
            middle = block_width // 2
            totals = [totals[0][:, :middle], totals[0][:, middle:]]
        low, high = (t.astype(BF) for t in totals)
        away = jnp.where(bits[0] == 1, low, high)
        kept = jnp.where(bits[0] == 1, high, low)
        turn.extend([away, kept])
        return kept, swap("dp", masks[0])(away)

    def halve(state, k):
        kept, came = state
        value = kept.astype(F32) + ordered(came).astype(F32)
        half = value.shape[0] // 2
        away = lax.dynamic_slice_in_dim(value, (1 - bits[k]) * half, half, 0).astype(BF)
        kept = lax.dynamic_slice_in_dim(value, bits[k] * half, half, 0).astype(BF)
        turn.extend([away, kept])
        return kept, swap("dp", masks[k])(away)

    def join(state, k):
        kept, came = state
        came = ordered(came)
        if k == len(masks) - 1:
            value = (kept.astype(F32) + came.astype(F32)).astype(BF)
        else:
            value = jnp.where(
                bits[k + 1] == 1,
                jnp.concatenate([came, kept], axis=0),
                jnp.concatenate([kept, came], axis=0),
            )
        turn.extend([value])
        return value, swap("dp", masks[k])(value)

    def last_join(state):
        value, came = state
        low = jnp.where(bits[0] == 1, came, value)
        high = jnp.where(bits[0] == 1, value, came)
        return jnp.concatenate([low, high], axis=1).astype(F32)

    def steps_of(pair):
        state = total_of(*pair)
        yield
        for k in range(1, len(masks)):
            state = halve(state, k)
            yield
        for k in reversed(range(len(masks))):
            state = join(state, k)
            yield
        yield last_join(state)

    down_pair = grads_of([low_t], [[u[0]] for u in units])
    down_near = held(down_near, *turn)
    down_near.update(forward_far(down_near))
    down_pieces = [line_of(down_near, line) for line in range(lines)]
    down_got = send_first(down_pair)

    back = []
    for line in range(lines):
        hidden, slope = units[line]
        pieces = up_pieces[line], down_pieces[line]
        back.append(done(mlp_back(ordered(low), hidden, slope, *pieces, steps), 0))
    grad_middle, grad_middle_low, grad_middle_t, second_sums = done(
        second_norm_back(
            ordered(middle), [b[3] for b in back], low, row_of(second_gain), meta, places
        ),
        0,
    )
    down_got = send_second(down_pair, down_got)
    grads = [None] * lines

    def back_of(line):
        qkv, _, probs, inverses, _ = forward[line]
        grads[line] = done(
            attend_back(
                ordered(grad_middle_low), attn_pieces[line], qkv, probs, inverses, steps
            ),
            0,
        )

    back_of(lines - 1)
    down_steps = steps_of((down_pair, down_got))
    next(down_steps)
    up_pair = grads_of([normed_two_t], [[b[0]] for b in back])
    up_got = send_first(up_pair)
    next(down_steps)
    for line in reversed(range(lines - 1)):
        back_of(line)
    up_got = send_second(up_pair, up_got)
    next(down_steps)
    attn_pair = grads_of(
        [normed_one_t, grad_middle_t],
        [[grads[line][0], forward[line][1]] for line in range(lines)],
    )
    attn_got = send_first(attn_pair)
    up_steps_left = steps_of((up_pair, up_got))
    next(up_steps_left)
    next(down_steps)
    output, input_grad, first_sums = done(
        finish(
            ordered(inputs),
            middle,
            [b[2] for b in back],
            grad_middle,
            [g[2] for g in grads],
            keep,
            row_of(first_gain),
            row_of(down_bias),
            meta,
            places,
        ),
        0,
    )
    next(up_steps_left)
    attn_got = send_second(attn_pair, attn_got)
    next(up_steps_left)
    attn_steps = steps_of((attn_pair, attn_got))
    next(attn_steps)
    *_, down_total = down_steps
    *_, up_total = up_steps_left
    *_, attn_total = attn_steps

    def in_order(values):
        stacked = jnp.stack(values)
        index = jnp.bitwise_xor(member, jnp.arange(groups, dtype=jnp.int32))
        return jnp.take(stacked, index, axis=0)

    unit_sums = jnp.concatenate([b[1] for b in back], axis=1).reshape(groups, -1)
    unit_sums = in_order(list(unit_sums))
    head_sums = jnp.concatenate([g[1] for g in grads], axis=1)
    head_sums = in_order(list(head_sums.reshape(groups, halves, 3, head_part)))
    query_sums = head_sums[:, :, 0].reshape(-1)
    value_sums = head_sums[:, :, 2].reshape(-1)
    vector = jnp.concatenate(
        [
            second_sums.reshape(-1),
            first_sums.reshape(-1),
            unit_sums.reshape(-1),
            query_sums,
            value_sums,
        ]
    ).reshape(-1, LANES)
    for axis, size in (("narrow", places), ("wide", groups), ("dp", copies)):
        mask = 1
        while mask < size:
            vector = vector + swap(axis, mask)(vector)
            mask *= 2
    vector = vector.reshape(-1)
    piece = lambda k: vector[k * width : (k + 1) * width]
    at = 6 * width
    units_all = hidden_width * groups
    line = member * places + place
    share = units_all // (groups * places)
    up_bias_grad = lax.dynamic_slice_in_dim(vector, at + line * share, share)
    at += units_all
    share = width // (groups * places)
    qv_bias_grad = jnp.stack(
        [
            lax.dynamic_slice_in_dim(vector, at + k * width + line * share, share)
            for k in range(2)
        ]
    )

    attn_total = attn_total.reshape(part, halves, 4, head_part)
    qkv_grad = attn_total[:, :, :3].transpose(0, 2, 1, 3).reshape(part, 3, part_width)
    out_grad = attn_total[:, :, 3].reshape(part, part_width).T
    return (
        output,
        input_grad,
        piece(4),
        piece(5),
        qkv_grad,
        qv_bias_grad,
        out_grad,
        piece(2),
        piece(0),
        piece(1),
        up_total,
        up_bias_grad,
        down_total.T,
        piece(3),
    )


def solution(mesh):
    placed = (
        P(("dp", "wide", "narrow"), None),
        P(("dp", "wide", "narrow")),
        P(),
        P(),
        P("narrow", None, "wide"),
        P(None, "wide"),
        P("wide", "narrow"),
        P(),
        P(),
        P(),
        P("narrow", "wide"),
        P("wide"),
        P("wide", "narrow"),
        P(),
        P(("dp", "wide", "narrow"), None),
    )
    return jax.shard_map(
        shards,
        mesh=mesh,
        in_specs=placed,
        out_specs=(
            P(("dp", "wide", "narrow"), None),
            P(("dp", "wide", "narrow"), None),
            P(),
            P(),
            P("narrow", None, "wide"),
            P(None, ("wide", "narrow")),
            P("wide", "narrow"),
            P(),
            P(),
            P(),
            P("narrow", "wide"),
            P(("wide", "narrow")),
            P("wide", "narrow"),
            P(),
        ),
        check_vma=False,
    )
```

```python
from functools import partial

import jax
import jax.numpy as jnp
import numpy as np
from jax import lax
from jax.experimental import pallas as pl
from jax.experimental.pallas import tpu as pltpu
from jax.sharding import PartitionSpec as P

HD = 64
LEN = 512
LANES = 128
EPSILON = 1e-06
MASKED = -1e30
SQRT_HALF = 0.7071067811865476
DENSITY_SCALE = 0.3989422804014327
BF = jnp.bfloat16
F32 = jnp.float32
MIB = 1 << 20

COSTS = {
    "turned": 2,
    "first_norm": 5,
    "attend": 11,
    "second_norm": 5,
    "up": 6,
    "weight_grads": 10,
    "mlp_back": 13,
    "second_norm_back": 6,
    "attend_back": 14,
    "finish": 8,
}
COST_UNIT = 0.3 * 3.69e6

NN = (((1,), (0,)), ((), ()))
NT = (((1,), (1,)), ((), ()))


def dot(left, right, dims=NN):
    return lax.dot_general(left, right, dims, preferred_element_type=F32)


def call(body, grid, ins, outs, operands, scratch=(), flops=0, name=None, vmem=36, tables=0):
    operands = [
        o.value
        if isinstance(o, Near)
        else o
        if o.size * o.dtype.itemsize < MIB // 4
        else pltpu.with_memory_space_constraint(o, pltpu.HBM)
        for o in operands
    ]
    return pl.pallas_call(
        body,
        out_shape=[o for _, o in outs],
        grid_spec=pltpu.PrefetchScalarGridSpec(
            num_scalar_prefetch=tables,
            grid=grid,
            in_specs=ins,
            out_specs=[s for s, _ in outs],
            scratch_shapes=list(scratch),
        ),
        compiler_params=pltpu.CompilerParams(vmem_limit_bytes=vmem * MIB),
        cost_estimate=pl.CostEstimate(
            flops=0, bytes_accessed=int(COSTS[name] * COST_UNIT), transcendentals=0
        ),
        name=name,
    )(*operands)


def after(value, *others):
    return lax.optimization_barrier((value, *others))[0]


class Near:
    def __init__(self, value):
        self.value, self.shape, self.dtype = value, value.shape, value.dtype


def shape(dims, dtype):
    return jax.ShapeDtypeStruct(dims, dtype)


def far_shape(dims, dtype):
    return pltpu.HBM(dims, dtype)


def columns(meta, ref, places, width):
    return jnp.concatenate(
        [ref[:, pl.ds(pl.multiple_of(meta[r], width), width)] for r in range(places)], axis=1
    )


def norm_stats(values):
    average = jnp.mean(values, axis=-1, keepdims=True)
    centred = values - average
    variance = jnp.mean(centred * centred, axis=-1, keepdims=True)
    scaled = lax.rsqrt(variance + EPSILON)
    return centred * scaled, scaled


def norm_back(upstream, gain, normal, scaled):
    inner = upstream * gain
    first_term = jnp.mean(inner, axis=-1, keepdims=True)
    second_term = jnp.mean(inner * normal, axis=-1, keepdims=True)
    return scaled * (inner - first_term - normal * second_term)


def turned(array, dtype):
    rows, width = array.shape
    block = min(512, max(rows, width))

    def body(array, out):
        out[...] = array[...].astype(F32).T.astype(dtype)

    if rows > width:
        spec = pl.BlockSpec((block, width), lambda i: (i, 0))
        out = pl.BlockSpec((width, block), lambda i: (0, i))
    else:
        spec = pl.BlockSpec((rows, block), lambda i: (0, i))
        out = pl.BlockSpec((block, rows), lambda i: (i, 0))
    return call(
        body,
        (max(rows, width) // block,),
        [spec],
        [(out, far_shape((width, rows), dtype))],
        (array,),
        name="turned",
    )[0]


def first_norm(inputs, cotangent, keep, gain, shift, meta, places):
    rows, width = inputs.shape
    block = 128
    part = width // places

    def body(meta, x, cot, keep, gain, shift, normed, normed_t, low, low_t):
        normal, _ = norm_stats(columns(meta, x, places, part).astype(F32))
        out = normal * columns(meta, gain, places, part) + columns(meta, shift, places, part)
        normed[...] = out.astype(BF)
        normed_t[...] = out.T.astype(BF)
        grad = columns(meta, cot, places, part).astype(F32) * keep[...]
        low[...] = grad.astype(BF)
        low_t[...] = grad.T.astype(BF)

    tall = pl.BlockSpec((block, width), lambda i, *_: (i, 0))
    wide = pl.BlockSpec((width, block), lambda i, *_: (0, i))
    vector = pl.BlockSpec((1, width), lambda i, *_: (0, 0))
    mark = pl.BlockSpec((block, 1), lambda i, *_: (i, 0))
    return call(
        body,
        (rows // block,),
        [tall, tall, mark, vector, vector],
        [
            (tall, shape((rows, width), BF)),
            (wide, far_shape((width, rows), BF)),
            (tall, far_shape((rows, width), BF)),
            (wide, far_shape((width, rows), BF)),
        ],
        (meta, inputs, cotangent, keep, gain, shift),
        tables=1,
        name="first_norm",
    )


def tile_of(refs, step, steps):
    blocks = []
    for parts in refs:
        value = parts[0][...]
        for k in range(1, len(parts)):
            value = jnp.where(step >= k * (steps // len(parts)), parts[k][...], value)
        blocks.append(value)
    return jnp.concatenate(blocks, axis=0)


def tile_specs(pieces, width, steps):
    specs, operands, counts = [], [], []
    for parts in pieces:
        counts.append(len(parts))
        per = steps // len(parts)
        for k, array in enumerate(parts):
            specs.append(
                pl.BlockSpec(
                    (array.shape[0], width),
                    lambda j, *_, k=k, per=per: (0, jnp.clip(j - k * per, 0, per - 1)),
                )
            )
            operands.append(array)
    return specs, operands, counts


def regroup(refs, counts):
    grouped, at = [], 0
    for count in counts:
        grouped.append(refs[at : at + count])
        at += count
    return grouped


def attend(normed, pieces, bias, labels_col, labels_row, halves):
    rows, width = normed.shape
    total = sum(p.shape[1] for p in pieces[0])
    wide = total // halves
    part = wide // 4
    heads = part // HD
    specs, weights, counts = tile_specs(pieces, wide, halves)

    def body(normed, *refs):
        weight_refs = regroup(refs[: len(weights)], counts)
        bias, lc, lr, qkv, attended, probs, inverses, branch, mask = refs[len(weights) :]
        step = pl.program_id(0)

        @pl.when(step == 0)
        def _():
            mask[...] = jnp.where(lc[...] == lr[...], 0.0, MASKED)

        tile = tile_of(weight_refs, step, halves)
        projected = dot(normed[...], tile[:, : 3 * part]) + bias[...].astype(F32)
        low = projected.astype(BF)
        qkv[...] = low
        lane = lax.broadcasted_iota(jnp.int32, (1, LANES), 1)
        per = LANES // HD
        queries, keys, values = [], [], []
        for pair in range(part // LANES):
            at = pair * LANES
            queries.append(low[:, at : at + LANES] * jnp.asarray(HD**-0.5, BF))
            keys.append(low[:, part + at : part + at + LANES])
            values.append(low[:, 2 * part + at : 2 * part + at + LANES].T)

        def scores_of(head):
            pair, e = divmod(head, per)
            mine = (lane >= e * HD) & (lane < (e + 1) * HD)
            key = jnp.where(mine, keys[pair], jnp.zeros_like(keys[pair]))
            return dot(key, queries[pair], NT)

        coming, outs = scores_of(0), []
        for head in range(heads):
            scores = coming
            if head + 1 < heads:
                coming = scores_of(head + 1)
            pair, e = divmod(head, per)
            scores = scores + mask[...]
            weight = jnp.exp(scores - jnp.max(scores, axis=0, keepdims=True))
            inverse = 1.0 / jnp.sum(weight, axis=0, keepdims=True)
            prob = weight.astype(BF)
            probs[head] = prob
            inverses[0, head : head + 1, :] = inverse
            outs.append(dot(values[pair][e * HD : (e + 1) * HD], prob) * inverse)
            if e == per - 1:
                at = pair * LANES
                attended[:, at : at + LANES] = jnp.concatenate(outs, axis=0).T.astype(BF)
                outs = []
        product = dot(attended[...], tile[:, 3 * part :], NT)

        @pl.when(step == 0)
        def _():
            branch[...] = product

        @pl.when(step > 0)
        def _():
            branch[...] += product

    fixed = lambda *dims: pl.BlockSpec(dims, lambda j, *_: (0,) * len(dims))
    return call(
        body,
        (halves,),
        [fixed(rows, width)]
        + specs
        + [pl.BlockSpec((1, 3 * part), lambda j: (0, j)), fixed(rows, 1), fixed(1, rows)],
        [
            (pl.BlockSpec((rows, 3 * part), lambda j: (0, j)), far_shape((rows, halves * 3 * part), BF)),
            (pl.BlockSpec((rows, part), lambda j: (0, j)), far_shape((rows, halves * part), BF)),
            (
                pl.BlockSpec((heads, rows, rows), lambda j: (j, 0, 0)),
                far_shape((halves * heads, rows, rows), BF),
            ),
            (pl.BlockSpec((1, heads, rows), lambda j: (j, 0, 0)), shape((halves, heads, rows), F32)),
            (fixed(rows, width), shape((rows, width), F32)),
        ],
        (Near(normed), *weights, bias, labels_col, labels_row),
        scratch=[pltpu.VMEM((rows, rows), F32)],
        flops=2 * rows * width * total + halves * heads * 8 * rows * rows * HD,
        name="attend",
    )


def second_norm(inputs, branches, out_bias, gain, shift, meta, places):
    rows, width = inputs.shape
    block = 128
    part = width // places
    count = len(branches)

    def body(meta, x, *refs):
        bias, gain, shift, middle, normed, normed_t = refs[count:]
        value = columns(meta, x, places, part).astype(F32)
        total = refs[0][...]
        for ref in refs[1:count]:
            total = total + ref[...]
        value = value + total + columns(meta, bias, places, part)
        middle[...] = value
        normal, _ = norm_stats(value)
        out = normal * columns(meta, gain, places, part) + columns(meta, shift, places, part)
        normed[...] = out.astype(BF)
        normed_t[...] = out.T.astype(BF)

    tall = pl.BlockSpec((block, width), lambda i, *_: (i, 0))
    wide = pl.BlockSpec((width, block), lambda i, *_: (0, i))
    vector = pl.BlockSpec((1, width), lambda i, *_: (0, 0))
    return call(
        body,
        (rows // block,),
        [tall] * (1 + count) + [vector] * 3,
        [
            (tall, far_shape((rows, width), F32)),
            (tall, shape((rows, width), BF)),
            (wide, far_shape((width, rows), BF)),
        ],
        (meta, inputs, *map(Near, branches), out_bias, gain, shift),
        tables=1,
        name="second_norm",
    )


def tiles_of(gathered, groups, line, lines, steps):
    places, part, columns_all = gathered.shape[1:]
    per_line = groups // lines
    per = steps // per_line
    wide = columns_all // per

    def spec(r):
        def index(j, spots):
            y = line * per_line + lax.div(j, jnp.int32(per))
            return (spots[places + y], spots[r], 0, lax.rem(j, jnp.int32(per)))

        return pl.BlockSpec((1, 1, part, wide), index)

    return [spec(r) for r in range(places)], wide


def joined(refs):
    return jnp.concatenate([ref[0, 0] for ref in refs], axis=0)


def up(normed, gathered, bias, spots, line, lines, steps):
    rows, width = normed.shape
    groups, places = gathered.shape[:2]
    specs, wide = tiles_of(gathered, groups, line, lines, steps)
    total = wide * steps

    def body(spots, normed, *refs):
        bias, hidden, slope = refs[places:]
        before = dot(normed[...], joined(refs[:places])) + bias[...].astype(F32)
        below = 0.5 * (1.0 + lax.erf(before * SQRT_HALF))
        hidden[...] = (before * below).astype(BF)
        density = jnp.exp(before * before * -0.5) * DENSITY_SCALE
        slope[...] = (below + before * density).astype(BF)

    tall = pl.BlockSpec((rows, wide), lambda j, *_: (0, j))
    return call(
        body,
        (steps,),
        [pl.BlockSpec((rows, width), lambda j, *_: (0, 0))]
        + specs
        + [pl.BlockSpec((1, wide), lambda j, *_: (0, j))],
        [(tall, shape((rows, total), BF)), (tall, shape((rows, total), BF))],
        (spots, Near(normed), *[gathered] * places, bias),
        name="up",
        tables=1,
    )


def mlp_back(low, hidden, slope, up_all, down_pieces, spots, line, lines, steps):
    rows, width = low.shape
    groups, places = up_all.shape[:2]
    specs, wide = tiles_of(up_all, groups, line, lines, steps)
    total = wide * steps

    down_specs, down_weights, counts = tile_specs(down_pieces, wide, steps)
    count = len(down_weights)

    def body(spots, low, hidden, slope, *refs):
        before, sums, mlp, normed = refs[places + count :]
        step = pl.program_id(0)
        up_tile = joined(refs[:places])
        down_tile = tile_of(regroup(refs[places : places + count], counts), step, steps)
        grad = dot(low[...], down_tile) * slope[...].astype(F32)
        grad_low = grad.astype(BF)
        before[...] = grad_low
        sums[...] = jnp.sum(grad_low.astype(F32), axis=0, keepdims=True)
        product = dot(hidden[...], down_tile, NT)
        back = dot(grad_low, up_tile, NT)

        @pl.when(step == 0)
        def _():
            mlp[...] = product
            normed[...] = back

        @pl.when(step > 0)
        def _():
            mlp[...] += product
            normed[...] += back

    fixed = pl.BlockSpec((rows, width), lambda j, *_: (0, 0))
    tall = pl.BlockSpec((rows, wide), lambda j, *_: (0, j))
    return call(
        body,
        (steps,),
        [fixed, tall, tall] + specs + down_specs,
        [
            (tall, far_shape((rows, total), BF)),
            (pl.BlockSpec((1, wide), lambda j, *_: (0, j)), shape((1, total), F32)),
            (fixed, far_shape((rows, width), F32)),
            (fixed, shape((rows, width), F32)),
        ],
        (spots, low, Near(hidden), Near(slope), *[up_all] * places, *down_weights),
        name="mlp_back",
        tables=1,
    )


def second_norm_back(middle, backs, low, gain, meta, places):
    rows, width = middle.shape
    block = 128
    part = width // places
    count = len(backs)

    def body(meta, middle, low, *refs):
        gain, grad, grad_low, grad_t, sums = refs[count:]
        upstream = refs[0][...]
        for ref in refs[1:count]:
            upstream = upstream + ref[...]
        normal, scaled = norm_stats(middle[...])
        out = low[...].astype(F32)
        total = out + norm_back(upstream, columns(meta, gain, places, part), normal, scaled)
        grad[...] = total
        grad_low[...] = total.astype(BF)
        grad_t[...] = total.T.astype(BF)

        @pl.when(pl.program_id(0) == 0)
        def _():
            sums[...] = jnp.zeros_like(sums)

        for k, value in enumerate((upstream * normal, upstream, total, out)):
            added = jnp.sum(value, axis=0, keepdims=True)
            for r in range(places):
                spot = pl.ds(pl.multiple_of(meta[r], part), part)
                sums[k : k + 1, spot] += added[:, r * part : (r + 1) * part]

    tall = pl.BlockSpec((block, width), lambda i, *_: (i, 0))
    wide = pl.BlockSpec((width, block), lambda i, *_: (0, i))
    vector = pl.BlockSpec((1, width), lambda i, *_: (0, 0))
    return call(
        body,
        (rows // block,),
        [tall, tall] + [tall] * count + [vector],
        [
            (tall, far_shape((rows, width), F32)),
            (tall, shape((rows, width), BF)),
            (wide, far_shape((width, rows), BF)),
            (pl.BlockSpec((4, width), lambda i, *_: (0, 0)), shape((4, width), F32)),
        ],
        (meta, middle, low, *map(Near, backs), gain),
        tables=1,
        name="second_norm_back",
    )


def attend_back(grad_low, pieces, qkv, probs, inverses, halves):
    rows, width = grad_low.shape
    total = sum(p.shape[1] for p in pieces[0])
    wide = total // halves
    part = wide // 4
    heads = part // HD
    specs, weights, counts = tile_specs(pieces, wide, halves)

    def body(grad_low, *refs):
        weight_refs = regroup(refs[: len(weights)], counts)
        qkv, probs, inverses, grads, sums, back = refs[len(weights) :]
        step = pl.program_id(0)
        tile = tile_of(weight_refs, step, halves)
        upstream = dot(grad_low[...], tile[:, 3 * part :]).astype(BF)
        lane = lax.broadcasted_iota(jnp.int32, (1, LANES), 1)
        factor = HD**-0.5
        per = LANES // HD
        queries, keys, values, ups = [], [], [], []
        for pair in range(part // LANES):
            at = pair * LANES
            queries.append(qkv[:, at : at + LANES] * jnp.asarray(factor, BF))
            key = qkv[:, part + at : part + at + LANES]
            keys.append((key * jnp.asarray(factor, BF)).T)
            values.append(qkv[:, 2 * part + at : 2 * part + at + LANES])
            up_t = upstream[:, at : at + LANES].T.astype(F32)
            scaled = [
                up_t[e * HD : (e + 1) * HD] * inverses[0, pair * per + e : pair * per + e + 1, :]
                for e in range(per)
            ]
            ups.append(jnp.concatenate(scaled, axis=0).T.astype(BF))

        def own(value, e):
            mine = (lane >= e * HD) & (lane < (e + 1) * HD)
            return jnp.where(mine, value, jnp.zeros_like(value))

        def first_of(head):
            pair, e = divmod(head, per)
            return dot(own(values[pair], e), ups[pair], NT)

        coming = first_of(0)
        for head in range(heads):
            pair, e = divmod(head, per)
            at = pair * LANES
            grad_probs = coming
            if head + 1 < heads:
                coming = first_of(head + 1)
            prob = probs[head].astype(F32)
            delta = jnp.sum(prob * grad_probs, axis=0, keepdims=True)
            delta = delta * inverses[0, head : head + 1, :]
            made = (prob * (grad_probs - delta)).astype(BF)
            if e == 0:
                grad_key = dot(made, own(queries[pair], e))
                grad_value = dot(probs[head], own(ups[pair], e))
                query_t = []
            else:
                grad_key = grad_key + dot(made, own(queries[pair], e))
                grad_value = grad_value + dot(probs[head], own(ups[pair], e))
            query_t.append(dot(keys[pair][e * HD : (e + 1) * HD], made))
            if e == per - 1:
                grad_query = jnp.concatenate(query_t, axis=0).T
                for c, grad in enumerate((grad_query, grad_key, grad_value)):
                    grads[:, c * part + at : c * part + at + LANES] = grad.astype(BF)
        made = grads[...]
        sums[...] = jnp.sum(made.astype(F32), axis=0, keepdims=True)
        product = dot(made, tile[:, : 3 * part], NT)

        @pl.when(step == 0)
        def _():
            back[...] = product

        @pl.when(step > 0)
        def _():
            back[...] += product

    fixed = pl.BlockSpec((rows, width), lambda j: (0, 0))
    wide_rows = pl.BlockSpec((rows, 3 * part), lambda j: (0, j))
    return call(
        body,
        (halves,),
        [fixed]
        + specs
        + [
            wide_rows,
            pl.BlockSpec((heads, rows, rows), lambda j: (j, 0, 0)),
            pl.BlockSpec((1, heads, rows), lambda j: (j, 0, 0)),
        ],
        [
            (wide_rows, shape((rows, halves * 3 * part), BF)),
            (pl.BlockSpec((1, 3 * part), lambda j: (0, j)), shape((1, halves * 3 * part), F32)),
            (fixed, far_shape((rows, width), F32)),
        ],
        (Near(grad_low), *weights, qkv, probs, inverses),
        flops=2 * rows * width * total + halves * heads * 8 * rows * rows * HD,
        name="attend_back",
    )


def finish(inputs, middle, mlps, grad_middle, backs, keep, gain, down_bias, meta, places):
    rows, width = inputs.shape
    block = 128
    part = width // places
    count = len(mlps)

    def body(meta, x, middle, grad, keep, *refs):
        gain, bias, output, input_grad, sums = refs[2 * count :]
        mlp, upstream = refs[0][...], refs[count][...]
        for k in range(1, count):
            mlp = mlp + refs[k][...]
            upstream = upstream + refs[count + k][...]
        out = (middle[...] + mlp + columns(meta, bias, places, part)) * keep[...]
        normal, scaled = norm_stats(columns(meta, x, places, part).astype(F32))
        back = grad[...] + norm_back(upstream, columns(meta, gain, places, part), normal, scaled)

        @pl.when(pl.program_id(0) == 0)
        def _():
            sums[...] = jnp.zeros_like(sums)

        gains = jnp.sum(upstream * normal, axis=0, keepdims=True)
        shifts = jnp.sum(upstream, axis=0, keepdims=True)
        for r in range(places):
            spot = pl.ds(pl.multiple_of(meta[r], part), part)
            here = slice(r * part, (r + 1) * part)
            output[:, spot] = out[:, here].astype(BF)
            input_grad[:, spot] = back[:, here].astype(BF)
            sums[0:1, spot] += gains[:, here]
            sums[1:2, spot] += shifts[:, here]

    tall = pl.BlockSpec((block, width), lambda i, *_: (i, 0))
    vector = pl.BlockSpec((1, width), lambda i, *_: (0, 0))
    mark = pl.BlockSpec((block, 1), lambda i, *_: (i, 0))
    return call(
        body,
        (rows // block,),
        [tall, tall, tall, mark] + [tall] * (2 * count) + [vector, vector],
        [
            (tall, shape((rows, width), BF)),
            (tall, shape((rows, width), BF)),
            (pl.BlockSpec((2, width), lambda i, *_: (0, 0)), shape((2, width), F32)),
        ],
        (meta, inputs, middle, grad_middle, keep, *mlps, *backs, gain, down_bias),
        tables=1,
        name="finish",
    )


def bundle_plan(members, halves):
    plan = {"x": [(1, y, 0) for y in members]}
    for y in members:
        if y:
            plan["keep", y] = [(0, y, 0)]
            if halves > 1:
                plan["y", y] = [(0, y, 1), (1, y, 1)]
    if 0 in members:
        if halves > 1:
            plan["far"] = [(1, 0, 1)]
        plan["own"] = [(0, 0, h) for h in range(halves)]
    return plan


def urgent(name):
    return name == "x" or name[0] == "y"


def alone(name):
    return urgent(name) or name == "far"


def weight_grads(plan, lefts, rights, blocks, halves):
    width, rows = lefts[0].shape
    part = width // 4
    lines = len(rights)
    first = min(y for made in plan.values() for _, y, _ in made) * halves // blocks
    spans = [array.shape[1] // blocks for array in rights[0]]
    wide = sum(spans)
    kinds = len(spans)
    order = []
    for made in plan.values():
        order += [block[1:] for block in made if block[1:] not in order]
    names = list(plan)
    rest = [block for name in names if not alone(name) for block in plan[name]]
    outs, joint = [], {}
    for core in range(2):
        for name in names:
            steps = [order.index(block[1:]) for block in plan[name]]
            joint[name] = len(set(steps)) == 1
            size = wide * (len(steps) if joint[name] else 1)
            starts = [] if joint[name] else steps[1:]

            def index(i, starts=starts):
                at = 0
                for start in starts:
                    at = at + (i >= start).astype(jnp.int32)
                return (0, at)

            if not core or alone(name):
                outs.append(
                    (pl.BlockSpec((part, size), index), far_shape((part, wide * len(steps)), BF))
                )
    whole = (part, wide * len(rest))
    outs.append((pl.BlockSpec(whole, lambda i: (0, 0)), far_shape(whole, BF)))

    def body(*refs):
        left_refs = refs[:kinds]
        right_refs = [refs[kinds + g * kinds : kinds + (g + 1) * kinds] for g in range(lines)]
        out_refs = refs[kinds + lines * kinds :]
        step = pl.program_id(0)
        for s, (y, h) in enumerate(order):

            @pl.when(step == s)
            def _(y=y, h=h):
                line = (y * halves + h) // blocks - first
                for r in range(4):
                    x, core = divmod(r, 2)
                    here = slice(r * part, (r + 1) * part)
                    products = [
                        dot(left_refs[k][here, :], right_refs[line][k][...]).astype(BF)
                        for k in range(kinds)
                    ]
                    value = jnp.concatenate(products, axis=1) if kinds > 1 else products[0]
                    if core and (x, y, h) in rest:
                        at = rest.index((x, y, h)) * wide
                        out_refs[-1][:, at : at + wide] = value
                        continue
                    sent = [name for name in names if alone(name)]
                    for n, name in enumerate(sent if core else names):
                        if (x, y, h) in plan[name]:
                            at = plan[name].index((x, y, h)) * wide if joint[name] else 0
                            out_refs[core * len(names) + n][:, at : at + wide] = value

    def right_map(g):
        flat = [y * halves + h for y, h in order]
        mine = [(s, at % blocks) for s, at in enumerate(flat) if at // blocks - first == g]
        def index(i):
            at = mine[0][1]
            for (s0, h0), (s1, h1) in zip(mine, mine[1:]):
                at = at + jnp.where(i > s0, h1 - h0, 0)
            return (0, at)
        return index
    ins = [pl.BlockSpec((width, rows), lambda i: (0, 0)) for _ in lefts]
    operands = list(lefts)
    for g in range(lines):
        for k in range(kinds):
            ins.append(pl.BlockSpec((rows, spans[k]), right_map(g)))
            operands.append(Near(rights[g][k]))
    made = call(body, (len(order),), ins, outs, operands, name="weight_grads")
    mine = dict(zip(names, made[: len(names)]))
    sent = [name for name in names if alone(name)]
    return mine, dict(zip([*sent, "rest"], made[len(names) :])), rest


def all_weight_grads(left, rights, spots, groups, places, blocks):
    width, rows = left.shape
    part = width // places
    lines = len(rights)
    wide = rights[0].shape[1] // blocks
    count = lines * blocks
    per = count // groups

    def body(spots, left, *refs):
        right_refs, out = refs[:lines], refs[lines]
        step = pl.program_id(0)
        for line in range(lines):

            @pl.when((step >= line * blocks) & (step < (line + 1) * blocks))
            def _(line=line):
                for r in range(places):
                    here = left[r * part : (r + 1) * part, :]
                    out[0, spots[r]] = dot(here, right_refs[line][...]).astype(BF)

    def right(line):
        return pl.BlockSpec(
            (rows, wide), lambda i, *_: (0, jnp.clip(i - line * blocks, 0, blocks - 1))
        )

    def index(i, spots):
        return (spots[places + lax.div(i, jnp.int32(per))], 0, 0, lax.rem(i, jnp.int32(per)))

    return call(
        body,
        (count,),
        [pl.BlockSpec((width, rows), lambda i, *_: (0, 0))] + [right(k) for k in range(lines)],
        [
            (
                pl.BlockSpec((1, places, part, wide), index),
                far_shape((groups, places, part, wide * per), BF),
            )
        ],
        (spots, left, *map(Near, rights)),
        name="weight_grads",
        tables=1,
    )[0]


def shards(
    inputs,
    segments,
    first_gain,
    first_shift,
    qkv_weight,
    qv_bias,
    out_weight,
    out_bias,
    second_gain,
    second_shift,
    up_weight,
    up_bias,
    down_weight,
    down_bias,
    cotangent,
):
    groups = lax.axis_size("wide")
    copies = lax.axis_size("dp")
    places = lax.axis_size("narrow")
    place = lax.axis_index("narrow")
    member = lax.axis_index("wide")
    rows, width = inputs.shape
    part_width = qkv_weight.shape[2]
    hidden_width = up_weight.shape[1]
    part = width // places
    halves = 2 if part_width >= 2 * LANES else 1
    head_part = part_width // halves
    lines = min(2, groups)
    per_line = groups // lines
    steps = per_line * halves
    unit_steps = max(per_line, per_line * hidden_width // 512)

    def members(line):
        return range(line * per_line, (line + 1) * per_line)

    def swap(axis, mask):
        size = lax.axis_size(axis)
        pairs = [(i, i ^ mask) for i in range(size)]
        return lambda value: lax.ppermute(value, axis, pairs)

    core = swap("narrow", 1)
    over_x = swap("narrow", 2)
    over_y = [None] + [swap("wide", m) for m in range(1, groups)]

    spots = jnp.concatenate(
        [
            jnp.bitwise_xor(place, jnp.arange(places, dtype=jnp.int32)),
            jnp.bitwise_xor(member, jnp.arange(groups, dtype=jnp.int32)),
        ]
    )
    meta = spots[:places] * part
    row_of = lambda vector: vector.astype(F32).reshape(1, -1)
    keep = (segments >= 0).astype(F32).reshape(rows, 1)
    labels_col = segments.reshape(rows, 1)
    labels_row = segments.reshape(1, rows)

    three = qkv_weight.reshape(part, 3, halves, head_part)
    out_t = out_weight.T.reshape(part, 1, halves, head_part)
    packed = jnp.concatenate([three, out_t], axis=1).transpose(0, 2, 1, 3)
    packed = packed.reshape(part, 4 * part_width)
    small = jnp.concatenate([qv_bias.reshape(-1), up_bias]).reshape(1, -1)
    down_t = turned(down_weight, BF)

    def split(array):
        wide = array.shape[1] // halves
        return [array[:, h * wide : (h + 1) * wide] for h in range(halves)]

    def reach(own, *others):
        ready = after(own, *others) if others else own
        near = {(0, 0): [own], (1, 0): [over_x(ready)]}
        for y in range(1, groups):
            near[0, y] = [over_y[y](ready)]
        return near

    passed = []

    def forward_far(near):
        made = {}
        for y in range(1, groups):
            sent = [split(near[0, y][0])[0]]
            made[1, y] = [over_x(sent[0])]
            if halves > 1:
                sent.append(split(near[1, 0][0])[1])
                made[1, y].append(over_y[y](sent[1]))
            passed.extend(sent)
        return made

    def line_of(near, line):
        made = []
        for x in range(2):
            parts = [array for y in members(line) for array in near[x, y]]
            made.append(parts)
            made.append([core(array) for array in parts])
        return made

    small_all = [small] + [over_y[y](small) for y in range(1, groups)]

    turn = []

    def ordered(value, *others):
        return after(value, *turn, *others) if turn or others else value

    def done(made, key):
        turn[:] = [made[key]]
        return made

    def first_stage(near):
        return [near[1, 0][0]] + [near[0, y][0] for y in range(1, groups)]

    def held(near, *others):
        return {
            key: value if key == (0, 0) else [after(array, *others) for array in value]
            for key, value in near.items()
        }

    def all_of(weight):
        made = lax.all_gather(weight, ("wide", "narrow"), axis=0)
        return made.reshape(groups, places, *weight.shape)

    attn_near = reach(packed)
    normed_one, normed_one_t, low, low_t = done(
        first_norm(
            inputs, cotangent, keep, row_of(first_gain), row_of(first_shift), meta, places
        ),
        0,
    )
    attn_near = held(attn_near, *turn)
    up_all = all_of(after(up_weight, *first_stage(attn_near)))

    def qkv_bias(values):
        query = values[:, :part_width].reshape(halves, 1, head_part)
        value = values[:, part_width : 2 * part_width].reshape(halves, 1, head_part)
        return jnp.concatenate([query, jnp.zeros_like(query), value], axis=1).reshape(1, -1)

    forward = []
    attn_far = forward_far(attn_near)
    down_near = reach(down_t, *turn, *passed)
    first = {key: attn_far[key] for key in attn_far if key[1] < per_line}
    attn_pieces = [line_of(attn_near | first, 0)]
    for line in range(lines):
        if line:
            attn_near = held(attn_near | attn_far, *turn)
            attn_pieces.append(line_of(attn_near, line))
        bias = jnp.concatenate([qkv_bias(small_all[y]) for y in members(line)], axis=1)
        forward.append(
            done(
                attend(
                    ordered(normed_one, down_t), attn_pieces[line], bias, labels_col, labels_row, steps
                ),
                1,
            )
        )
    middle, normed_two, normed_two_t = done(
        second_norm(
            ordered(inputs),
            [f[4] for f in forward],
            row_of(out_bias),
            row_of(second_gain),
            row_of(second_shift),
            meta,
            places,
        ),
        0,
    )
    down_near = held(down_near, *turn)
    turn.extend(first_stage(down_near))
    down_far = forward_far(down_near)
    units = []
    for line in range(lines):
        bias = [small_all[y][:, 2 * part_width :] for y in members(line)]
        bias = jnp.concatenate(bias, axis=1)
        units.append(
            done(up(ordered(normed_two), up_all, bias, spots, line, lines, unit_steps), 0)
        )

    down_far = held(down_far, *turn)
    turn.extend(array for arrays in down_far.values() for array in arrays)
    block_width = 4 * head_part

    def cut(array, k):
        return array[:, k * block_width : (k + 1) * block_width].astype(F32)

    def grads_of(lefts, rights, ys=range(groups)):
        plan = bundle_plan(ys, halves)
        lefts = [ordered(lefts[0])] + lefts[1:]
        mine, other, rest = weight_grads(plan, lefts, rights, steps, halves)
        turn[:] = [next(iter(mine.values()))]
        came = {name: core(value) for name, value in other.items()}
        at = {}
        for name in mine:
            if not alone(name):
                at[name] = rest.index(plan[name][0]), len(plan[name])
        return ys, mine, came, at

    def both(made, name):
        _, mine, came, at = made
        if name in came:
            return mine[name].astype(F32) + ordered(came[name]).astype(F32)
        first, count = at[name]
        last = first + count
        came = ordered(came["rest"])[:, first * block_width : last * block_width]
        return mine[name].astype(F32) + came.astype(F32)

    def send_first(made):
        ys, mine = made[:2]
        sums = {name: both(made, name).astype(BF) for name in mine if urgent(name)}
        turn.extend(sums.values())
        got = {}
        for name, value in sums.items():
            if name == "x":
                from_x = over_x(value)
                got.update({("x", y): (from_x, k) for k, y in enumerate(ys)})
            else:
                got[name] = over_y[name[1]](value)
        return got

    def send_near(made, got, late):
        for y in made[0]:
            if y:
                array, k = got["x", y]
                value = (both(made, ("keep", y)) + cut(ordered(array), k)).astype(BF)
                turn.append(value)
                late[y] = over_y[y](value)

    def send_far(made, got, late):
        if halves > 1:
            value = both(made, "far")
            for y in range(1, groups):
                value = value + cut(ordered(got["y", y]), 1)
            value = value.astype(BF)
            turn.append(value)
            late["far"] = over_x(value)

    def total_of(parts, got, late):
        own = [both(made, "own") for made in parts if 0 in made[0]][0]
        late = {key: ordered(value).astype(F32) for key, value in late.items()}
        totals = [own[:, h * block_width : (h + 1) * block_width] for h in range(halves)]
        totals[0] = totals[0] + cut(*got["x", 0])
        for y in range(1, groups):
            totals[0] = totals[0] + late[y]
            if halves > 1:
                totals[1] = totals[1] + cut(got["y", y], 0)
        if halves > 1:
            totals[1] = totals[1] + late["far"]
        return totals

    copy_index = lax.axis_index("dp")
    masks = [1 << k for k in range(copies.bit_length() - 1)]
    bits = [(copy_index // mask) % 2 for mask in masks]

    def first_halve(totals):
        if len(totals) == 1:
            middle = block_width // 2
            totals = [totals[0][:, :middle], totals[0][:, middle:]]
        low, high = (t.astype(BF) for t in totals)
        away = jnp.where(bits[0] == 1, low, high)
        kept = jnp.where(bits[0] == 1, high, low)
        turn.extend([away, kept])
        return kept, swap("dp", masks[0])(away)

    def halve(state, k):
        kept, came = state
        value = kept.astype(F32) + ordered(came).astype(F32)
        half = value.shape[0] // 2
        away = lax.dynamic_slice_in_dim(value, (1 - bits[k]) * half, half, 0).astype(BF)
        kept = lax.dynamic_slice_in_dim(value, bits[k] * half, half, 0).astype(BF)
        turn.extend([away, kept])
        return kept, swap("dp", masks[k])(away)

    def join(state, k):
        kept, came = state
        came = ordered(came)
        if k == len(masks) - 1:
            value = (kept.astype(F32) + came.astype(F32)).astype(BF)
        else:
            value = jnp.where(
                bits[k + 1] == 1,
                jnp.concatenate([came, kept], axis=0),
                jnp.concatenate([kept, came], axis=0),
            )
        turn.extend([value])
        return value, swap("dp", masks[k])(value)

    def last_join(state, dtype=F32):
        value, came = state
        low = jnp.where(bits[0] == 1, came, value)
        high = jnp.where(bits[0] == 1, value, came)
        return jnp.concatenate([low, high], axis=1).astype(dtype)

    def vector_steps(vector):
        for axis, size in (("narrow", places), ("wide", groups), ("dp", copies)):
            mask = 1
            while mask < size:
                vector = vector + swap(axis, mask)(vector)
                yield vector
                mask *= 2

    first = {key: down_far[key] for key in down_far if key[1] < per_line}
    down_pieces = [line_of(down_near | first, 0)]
    down_grad = all_weight_grads(
        ordered(low_t), [u[0] for u in units], spots, groups, places, steps
    )
    turn[:] = [down_grad]
    down_pieces += [line_of(down_near | down_far, line) for line in range(1, lines)]
    down_grad = lax.psum_scatter(
        down_grad.reshape(groups * places, part, hidden_width),
        ("wide", "narrow"),
        scatter_dimension=0,
        tiled=True,
    )[0]
    back = []
    for line in range(lines):
        hidden, slope = units[line]
        back.append(
            done(
                mlp_back(
                    ordered(low),
                    hidden,
                    slope,
                    up_all,
                    down_pieces[line],
                    spots,
                    line,
                    lines,
                    unit_steps,
                ),
                0,
            )
        )
    up_made = grads_of([normed_two_t], [[b[0]] for b in back])
    grad_middle, grad_middle_low, grad_middle_t, second_sums = done(
        second_norm_back(
            ordered(middle), [b[3] for b in back], low, row_of(second_gain), meta, places
        ),
        0,
    )
    up_got = send_first(up_made)
    grads = [None] * lines

    def back_of(line):
        qkv, _, probs, inverses, _ = forward[line]
        grads[line] = done(
            attend_back(
                ordered(grad_middle_low), attn_pieces[line], qkv, probs, inverses, steps
            ),
            0,
        )

    attn_made, attn_got, attn_late, up_late = [], {}, {}, {}

    def attn_grads(line):
        rights = [[grads[line][0], forward[line][1]]]
        made = grads_of([normed_one_t, grad_middle_t], rights, members(line))
        attn_made.append(made)
        return made

    back_of(lines - 1)
    down_state = first_halve(
        [down_grad[:, : hidden_width // 2], down_grad[:, hidden_width // 2 :]]
    )
    for line in reversed(range(1, lines)):
        made = attn_grads(line)
        if line == lines - 1:
            send_near(up_made, up_got, up_late)
            send_far(up_made, up_got, up_late)
            for k in range(1, len(masks)):
                down_state = halve(down_state, k)
        back_of(line - 1)
        attn_got |= send_first(made)
    for k in reversed(range(1, len(masks))):
        down_state = join(down_state, k)
    up_state = first_halve(total_of([up_made], up_got, up_late))
    output, input_grad, first_sums = done(
        finish(
            ordered(inputs),
            middle,
            [b[2] for b in back],
            grad_middle,
            [g[2] for g in grads],
            keep,
            row_of(first_gain),
            row_of(down_bias),
            meta,
            places,
        ),
        0,
    )
    def in_order(values):
        stacked = jnp.stack(values)
        index = jnp.bitwise_xor(member, jnp.arange(groups, dtype=jnp.int32))
        return jnp.take(stacked, index, axis=0)

    unit_sums = jnp.concatenate([b[1] for b in back], axis=1).reshape(groups, -1)
    unit_sums = in_order(list(unit_sums))
    head_sums = jnp.concatenate([g[1] for g in grads], axis=1)
    head_sums = in_order(list(head_sums.reshape(groups, halves, 3, head_part)))
    query_sums = head_sums[:, :, 0].reshape(-1)
    value_sums = head_sums[:, :, 2].reshape(-1)
    vector = jnp.concatenate(
        [
            second_sums.reshape(-1),
            first_sums.reshape(-1),
            unit_sums.reshape(-1),
            query_sums,
            value_sums,
        ]
    ).reshape(-1, LANES)
    for made in attn_made:
        send_near(made, attn_got, attn_late)
    down_state = join(down_state, 0)
    made = attn_grads(0)
    up_state = halve(up_state, 1)
    attn_got |= send_first(made)
    send_near(made, attn_got, attn_late)
    send_far(made, attn_got, attn_late)
    for k in range(2, len(masks)):
        up_state = halve(up_state, k)
    for k in reversed(range(1, len(masks))):
        up_state = join(up_state, k)
    for vector in vector_steps(ordered(vector)):
        pass
    down_total = last_join(down_state, BF)
    state = first_halve(total_of(attn_made, attn_got, attn_late))
    up_state = join(up_state, 0)
    for k in range(1, len(masks)):
        state = halve(state, k)
    for k in reversed(range(len(masks))):
        state = join(state, k)
    attn_total, up_total = last_join(state), last_join(up_state)
    vector = vector.reshape(-1)
    piece = lambda k: vector[k * width : (k + 1) * width]
    at = 6 * width
    units_all = hidden_width * groups
    line = member * places + place
    share = units_all // (groups * places)
    up_bias_grad = lax.dynamic_slice_in_dim(vector, at + line * share, share)
    at += units_all
    share = width // (groups * places)
    qv_bias_grad = jnp.stack(
        [
            lax.dynamic_slice_in_dim(vector, at + k * width + line * share, share)
            for k in range(2)
        ]
    )

    spans = [attn_total[:, k * head_part : (k + 1) * head_part] for k in range(4 * halves)]
    spans = [jnp.concatenate(spans[k::4], axis=1) for k in range(4)]
    qkv_grad = jnp.stack(spans[:3]).transpose(1, 0, 2)
    out_grad = turned(spans[3], F32)
    return (
        output,
        input_grad,
        piece(4),
        piece(5),
        qkv_grad,
        qv_bias_grad,
        out_grad,
        piece(2),
        piece(0),
        piece(1),
        up_total,
        up_bias_grad,
        turned(down_total, F32),
        piece(3),
    )


def solution(mesh):
    placed = (
        P(("dp", "wide", "narrow"), None),
        P(("dp", "wide", "narrow")),
        P(),
        P(),
        P("narrow", None, "wide"),
        P(None, "wide"),
        P("wide", "narrow"),
        P(),
        P(),
        P(),
        P("narrow", "wide"),
        P("wide"),
        P("wide", "narrow"),
        P(),
        P(("dp", "wide", "narrow"), None),
    )
    return jax.shard_map(
        shards,
        mesh=mesh,
        in_specs=placed,
        out_specs=(
            P(("dp", "wide", "narrow"), None),
            P(("dp", "wide", "narrow"), None),
            P(),
            P(),
            P("narrow", None, "wide"),
            P(None, ("wide", "narrow")),
            P("wide", "narrow"),
            P(),
            P(),
            P(),
            P("narrow", "wide"),
            P(("wide", "narrow")),
            P("wide", "narrow"),
            P(),
        ),
        check_vma=False,
    )
```

```python
from functools import partial

import jax
import jax.numpy as jnp
import numpy as np
from jax import lax
from jax.experimental import pallas as pl
from jax.experimental.pallas import tpu as pltpu
from jax.sharding import PartitionSpec as P

HD = 64
LEN = 512
LANES = 128
EPSILON = 1e-06
MASKED = -1e30
SQRT_HALF = 0.7071067811865476
DENSITY_SCALE = 0.3989422804014327
BF = jnp.bfloat16
F32 = jnp.float32
MIB = 1 << 20

COSTS = {
    "turned": 2,
    "first_norm": 5,
    "attend": 11,
    "second_norm": 5,
    "up": 6,
    "weight_grads": 10,
    "mlp_back": 13,
    "second_norm_back": 6,
    "attend_back": 14,
    "finish": 8,
}
COST_UNIT = 0.3 * 3.69e6

NN = (((1,), (0,)), ((), ()))
NT = (((1,), (1,)), ((), ()))


def dot(left, right, dims=NN):
    return lax.dot_general(left, right, dims, preferred_element_type=F32)


def call(body, grid, ins, outs, operands, scratch=(), flops=0, name=None, vmem=36, tables=0):
    operands = [
        o.value
        if isinstance(o, Near)
        else o
        if o.size * o.dtype.itemsize < MIB // 4
        else pltpu.with_memory_space_constraint(o, pltpu.HBM)
        for o in operands
    ]
    return pl.pallas_call(
        body,
        out_shape=[o for _, o in outs],
        grid_spec=pltpu.PrefetchScalarGridSpec(
            num_scalar_prefetch=tables,
            grid=grid,
            in_specs=ins,
            out_specs=[s for s, _ in outs],
            scratch_shapes=list(scratch),
        ),
        compiler_params=pltpu.CompilerParams(vmem_limit_bytes=vmem * MIB),
        cost_estimate=pl.CostEstimate(
            flops=0, bytes_accessed=int(COSTS[name] * COST_UNIT), transcendentals=0
        ),
        name=name,
    )(*operands)


def after(value, *others):
    return lax.optimization_barrier((value, *others))[0]


class Near:
    def __init__(self, value):
        self.value, self.shape, self.dtype = value, value.shape, value.dtype


def shape(dims, dtype):
    return jax.ShapeDtypeStruct(dims, dtype)


def far_shape(dims, dtype):
    return pltpu.HBM(dims, dtype)


def columns(meta, ref, places, width):
    return jnp.concatenate(
        [ref[:, pl.ds(pl.multiple_of(meta[r], width), width)] for r in range(places)], axis=1
    )


def norm_stats(values):
    average = jnp.mean(values, axis=-1, keepdims=True)
    centred = values - average
    variance = jnp.mean(centred * centred, axis=-1, keepdims=True)
    scaled = lax.rsqrt(variance + EPSILON)
    return centred * scaled, scaled


def norm_back(upstream, gain, normal, scaled):
    inner = upstream * gain
    first_term = jnp.mean(inner, axis=-1, keepdims=True)
    second_term = jnp.mean(inner * normal, axis=-1, keepdims=True)
    return scaled * (inner - first_term - normal * second_term)


def turned(array, dtype):
    rows, width = array.shape
    block = min(512, max(rows, width))

    def body(array, out):
        out[...] = array[...].astype(F32).T.astype(dtype)

    if rows > width:
        spec = pl.BlockSpec((block, width), lambda i: (i, 0))
        out = pl.BlockSpec((width, block), lambda i: (0, i))
    else:
        spec = pl.BlockSpec((rows, block), lambda i: (0, i))
        out = pl.BlockSpec((block, rows), lambda i: (i, 0))
    return call(
        body,
        (max(rows, width) // block,),
        [spec],
        [(out, far_shape((width, rows), dtype))],
        (array,),
        name="turned",
    )[0]


def first_norm(inputs, cotangent, keep, gain, shift, meta, places):
    rows, width = inputs.shape
    block = 128
    part = width // places

    def body(meta, x, cot, keep, gain, shift, normed, normed_t, low, low_t):
        normal, _ = norm_stats(columns(meta, x, places, part).astype(F32))
        out = normal * columns(meta, gain, places, part) + columns(meta, shift, places, part)
        normed[...] = out.astype(BF)
        normed_t[...] = out.T.astype(BF)
        grad = columns(meta, cot, places, part).astype(F32) * keep[...]
        low[...] = grad.astype(BF)
        low_t[...] = grad.T.astype(BF)

    tall = pl.BlockSpec((block, width), lambda i, *_: (i, 0))
    wide = pl.BlockSpec((width, block), lambda i, *_: (0, i))
    vector = pl.BlockSpec((1, width), lambda i, *_: (0, 0))
    mark = pl.BlockSpec((block, 1), lambda i, *_: (i, 0))
    return call(
        body,
        (rows // block,),
        [tall, tall, mark, vector, vector],
        [
            (tall, shape((rows, width), BF)),
            (wide, far_shape((width, rows), BF)),
            (tall, far_shape((rows, width), BF)),
            (wide, far_shape((width, rows), BF)),
        ],
        (meta, inputs, cotangent, keep, gain, shift),
        tables=1,
        name="first_norm",
    )


def tile_of(refs, step, steps):
    blocks = []
    for parts in refs:
        value = parts[0][...]
        for k in range(1, len(parts)):
            value = jnp.where(step >= k * (steps // len(parts)), parts[k][...], value)
        blocks.append(value)
    return jnp.concatenate(blocks, axis=0)


def tile_specs(pieces, width, steps):
    specs, operands, counts = [], [], []
    for parts in pieces:
        counts.append(len(parts))
        per = steps // len(parts)
        for k, array in enumerate(parts):
            specs.append(
                pl.BlockSpec(
                    (array.shape[0], width),
                    lambda j, *_, k=k, per=per: (0, jnp.clip(j - k * per, 0, per - 1)),
                )
            )
            operands.append(array)
    return specs, operands, counts


def regroup(refs, counts):
    grouped, at = [], 0
    for count in counts:
        grouped.append(refs[at : at + count])
        at += count
    return grouped


def attend(normed, pieces, bias, labels_col, labels_row, halves):
    rows, width = normed.shape
    total = sum(p.shape[1] for p in pieces[0])
    wide = total // halves
    part = wide // 4
    heads = part // HD
    specs, weights, counts = tile_specs(pieces, wide, halves)

    def body(normed, *refs):
        weight_refs = regroup(refs[: len(weights)], counts)
        bias, lc, lr, qkv, attended, probs, inverses, branch, mask = refs[len(weights) :]
        step = pl.program_id(0)

        @pl.when(step == 0)
        def _():
            mask[...] = jnp.where(lc[...] == lr[...], 0.0, MASKED)

        tile = tile_of(weight_refs, step, halves)
        projected = dot(normed[...], tile[:, : 3 * part]) + bias[...].astype(F32)
        low = projected.astype(BF)
        qkv[...] = low
        lane = lax.broadcasted_iota(jnp.int32, (1, LANES), 1)
        per = LANES // HD
        queries, keys, values = [], [], []
        for pair in range(part // LANES):
            at = pair * LANES
            queries.append(low[:, at : at + LANES] * jnp.asarray(HD**-0.5, BF))
            keys.append(low[:, part + at : part + at + LANES])
            values.append(low[:, 2 * part + at : 2 * part + at + LANES].T)

        def scores_of(head):
            pair, e = divmod(head, per)
            mine = (lane >= e * HD) & (lane < (e + 1) * HD)
            key = jnp.where(mine, keys[pair], jnp.zeros_like(keys[pair]))
            return dot(key, queries[pair], NT)

        coming, outs = scores_of(0), []
        for head in range(heads):
            scores = coming
            if head + 1 < heads:
                coming = scores_of(head + 1)
            pair, e = divmod(head, per)
            scores = scores + mask[...]
            weight = jnp.exp(scores - jnp.max(scores, axis=0, keepdims=True))
            inverse = 1.0 / jnp.sum(weight, axis=0, keepdims=True)
            prob = weight.astype(BF)
            probs[head] = prob
            inverses[0, head : head + 1, :] = inverse
            outs.append(dot(values[pair][e * HD : (e + 1) * HD], prob) * inverse)
            if e == per - 1:
                at = pair * LANES
                attended[:, at : at + LANES] = jnp.concatenate(outs, axis=0).T.astype(BF)
                outs = []
        product = dot(attended[...], tile[:, 3 * part :], NT)

        @pl.when(step == 0)
        def _():
            branch[...] = product

        @pl.when(step > 0)
        def _():
            branch[...] += product

    fixed = lambda *dims: pl.BlockSpec(dims, lambda j, *_: (0,) * len(dims))
    return call(
        body,
        (halves,),
        [fixed(rows, width)]
        + specs
        + [pl.BlockSpec((1, 3 * part), lambda j: (0, j)), fixed(rows, 1), fixed(1, rows)],
        [
            (pl.BlockSpec((rows, 3 * part), lambda j: (0, j)), far_shape((rows, halves * 3 * part), BF)),
            (pl.BlockSpec((rows, part), lambda j: (0, j)), far_shape((rows, halves * part), BF)),
            (
                pl.BlockSpec((heads, rows, rows), lambda j: (j, 0, 0)),
                far_shape((halves * heads, rows, rows), BF),
            ),
            (pl.BlockSpec((1, heads, rows), lambda j: (j, 0, 0)), shape((halves, heads, rows), F32)),
            (fixed(rows, width), shape((rows, width), F32)),
        ],
        (Near(normed), *weights, bias, labels_col, labels_row),
        scratch=[pltpu.VMEM((rows, rows), F32)],
        flops=2 * rows * width * total + halves * heads * 8 * rows * rows * HD,
        name="attend",
    )


def second_norm(inputs, branches, out_bias, gain, shift, meta, places):
    rows, width = inputs.shape
    block = 128
    part = width // places
    count = len(branches)

    def body(meta, x, *refs):
        bias, gain, shift, middle, normed, normed_t = refs[count:]
        value = columns(meta, x, places, part).astype(F32)
        total = refs[0][...]
        for ref in refs[1:count]:
            total = total + ref[...]
        value = value + total + columns(meta, bias, places, part)
        middle[...] = value
        normal, _ = norm_stats(value)
        out = normal * columns(meta, gain, places, part) + columns(meta, shift, places, part)
        normed[...] = out.astype(BF)
        normed_t[...] = out.T.astype(BF)

    tall = pl.BlockSpec((block, width), lambda i, *_: (i, 0))
    wide = pl.BlockSpec((width, block), lambda i, *_: (0, i))
    vector = pl.BlockSpec((1, width), lambda i, *_: (0, 0))
    return call(
        body,
        (rows // block,),
        [tall] * (1 + count) + [vector] * 3,
        [
            (tall, far_shape((rows, width), F32)),
            (tall, shape((rows, width), BF)),
            (wide, far_shape((width, rows), BF)),
        ],
        (meta, inputs, *map(Near, branches), out_bias, gain, shift),
        tables=1,
        name="second_norm",
    )


def tiles_of(gathered, groups, line, lines, steps):
    places, part, columns_all = gathered.shape[1:]
    per_line = groups // lines
    per = steps // per_line
    wide = columns_all // per

    def spec(r):
        def index(j, spots):
            y = line * per_line + lax.div(j, jnp.int32(per))
            return (spots[places + y], spots[r], 0, lax.rem(j, jnp.int32(per)))

        return pl.BlockSpec((1, 1, part, wide), index)

    return [spec(r) for r in range(places)], wide


def joined(refs):
    return jnp.concatenate([ref[0, 0] for ref in refs], axis=0)


def up(normed, gathered, bias, spots, line, lines, steps):
    rows, width = normed.shape
    groups, places = gathered.shape[:2]
    specs, wide = tiles_of(gathered, groups, line, lines, steps)
    total = wide * steps

    def body(spots, normed, *refs):
        bias, hidden, slope = refs[places:]
        before = dot(normed[...], joined(refs[:places])) + bias[...].astype(F32)
        below = 0.5 * (1.0 + lax.erf(before * SQRT_HALF))
        hidden[...] = (before * below).astype(BF)
        density = jnp.exp(before * before * -0.5) * DENSITY_SCALE
        slope[...] = (below + before * density).astype(BF)

    tall = pl.BlockSpec((rows, wide), lambda j, *_: (0, j))
    return call(
        body,
        (steps,),
        [pl.BlockSpec((rows, width), lambda j, *_: (0, 0))]
        + specs
        + [pl.BlockSpec((1, wide), lambda j, *_: (0, j))],
        [(tall, far_shape((rows, total), BF)), (tall, far_shape((rows, total), BF))],
        (spots, Near(normed), *[gathered] * places, bias),
        name="up",
        tables=1,
    )


def mlp_back(low, hidden, slope, up_all, down_pieces, spots, line, lines, steps):
    rows, width = low.shape
    groups, places = up_all.shape[:2]
    specs, wide = tiles_of(up_all, groups, line, lines, steps)
    total = wide * steps

    down_specs, down_weights, counts = tile_specs(down_pieces, wide, steps)
    count = len(down_weights)

    def body(spots, low, hidden, slope, *refs):
        before, sums, mlp, normed = refs[places + count :]
        step = pl.program_id(0)
        up_tile = joined(refs[:places])
        down_tile = tile_of(regroup(refs[places : places + count], counts), step, steps)
        grad = dot(low[...], down_tile) * slope[...].astype(F32)
        grad_low = grad.astype(BF)
        before[...] = grad_low
        sums[...] = jnp.sum(grad_low.astype(F32), axis=0, keepdims=True)
        product = dot(hidden[...], down_tile, NT)
        back = dot(grad_low, up_tile, NT)

        @pl.when(step == 0)
        def _():
            mlp[...] = product
            normed[...] = back

        @pl.when(step > 0)
        def _():
            mlp[...] += product
            normed[...] += back

    fixed = pl.BlockSpec((rows, width), lambda j, *_: (0, 0))
    tall = pl.BlockSpec((rows, wide), lambda j, *_: (0, j))
    return call(
        body,
        (steps,),
        [fixed, tall, tall] + specs + down_specs,
        [
            (tall, far_shape((rows, total), BF)),
            (pl.BlockSpec((1, wide), lambda j, *_: (0, j)), shape((1, total), F32)),
            (fixed, far_shape((rows, width), F32)),
            (fixed, shape((rows, width), F32)),
        ],
        (spots, low, hidden, slope, *[up_all] * places, *down_weights),
        name="mlp_back",
        tables=1,
    )


def second_norm_back(middle, backs, low, gain, meta, places):
    rows, width = middle.shape
    block = 128
    part = width // places
    count = len(backs)

    def body(meta, middle, low, *refs):
        gain, grad, grad_low, grad_t, sums = refs[count:]
        upstream = refs[0][...]
        for ref in refs[1:count]:
            upstream = upstream + ref[...]
        normal, scaled = norm_stats(middle[...])
        out = low[...].astype(F32)
        total = out + norm_back(upstream, columns(meta, gain, places, part), normal, scaled)
        grad[...] = total
        grad_low[...] = total.astype(BF)
        grad_t[...] = total.T.astype(BF)

        @pl.when(pl.program_id(0) == 0)
        def _():
            sums[...] = jnp.zeros_like(sums)

        for k, value in enumerate((upstream * normal, upstream, total, out)):
            added = jnp.sum(value, axis=0, keepdims=True)
            for r in range(places):
                spot = pl.ds(pl.multiple_of(meta[r], part), part)
                sums[k : k + 1, spot] += added[:, r * part : (r + 1) * part]

    tall = pl.BlockSpec((block, width), lambda i, *_: (i, 0))
    wide = pl.BlockSpec((width, block), lambda i, *_: (0, i))
    vector = pl.BlockSpec((1, width), lambda i, *_: (0, 0))
    return call(
        body,
        (rows // block,),
        [tall, tall] + [tall] * count + [vector],
        [
            (tall, far_shape((rows, width), F32)),
            (tall, shape((rows, width), BF)),
            (wide, far_shape((width, rows), BF)),
            (pl.BlockSpec((4, width), lambda i, *_: (0, 0)), shape((4, width), F32)),
        ],
        (meta, middle, low, *map(Near, backs), gain),
        tables=1,
        name="second_norm_back",
    )


def attend_back(grad_low, pieces, qkv, probs, inverses, halves):
    rows, width = grad_low.shape
    total = sum(p.shape[1] for p in pieces[0])
    wide = total // halves
    part = wide // 4
    heads = part // HD
    specs, weights, counts = tile_specs(pieces, wide, halves)

    def body(grad_low, *refs):
        weight_refs = regroup(refs[: len(weights)], counts)
        qkv, probs, inverses, grads, sums, back = refs[len(weights) :]
        step = pl.program_id(0)
        tile = tile_of(weight_refs, step, halves)
        upstream = dot(grad_low[...], tile[:, 3 * part :]).astype(BF)
        lane = lax.broadcasted_iota(jnp.int32, (1, LANES), 1)
        factor = HD**-0.5
        per = LANES // HD
        queries, keys, values, ups = [], [], [], []
        for pair in range(part // LANES):
            at = pair * LANES
            queries.append(qkv[:, at : at + LANES] * jnp.asarray(factor, BF))
            key = qkv[:, part + at : part + at + LANES]
            keys.append((key * jnp.asarray(factor, BF)).T)
            values.append(qkv[:, 2 * part + at : 2 * part + at + LANES])
            up_t = upstream[:, at : at + LANES].T.astype(F32)
            scaled = [
                up_t[e * HD : (e + 1) * HD] * inverses[0, pair * per + e : pair * per + e + 1, :]
                for e in range(per)
            ]
            ups.append(jnp.concatenate(scaled, axis=0).T.astype(BF))

        def own(value, e):
            mine = (lane >= e * HD) & (lane < (e + 1) * HD)
            return jnp.where(mine, value, jnp.zeros_like(value))

        def first_of(head):
            pair, e = divmod(head, per)
            return dot(own(values[pair], e), ups[pair], NT)

        coming = first_of(0)
        for head in range(heads):
            pair, e = divmod(head, per)
            at = pair * LANES
            grad_probs = coming
            if head + 1 < heads:
                coming = first_of(head + 1)
            prob = probs[head].astype(F32)
            delta = jnp.sum(prob * grad_probs, axis=0, keepdims=True)
            delta = delta * inverses[0, head : head + 1, :]
            made = (prob * (grad_probs - delta)).astype(BF)
            if e == 0:
                grad_key = dot(made, own(queries[pair], e))
                grad_value = dot(probs[head], own(ups[pair], e))
                query_t = []
            else:
                grad_key = grad_key + dot(made, own(queries[pair], e))
                grad_value = grad_value + dot(probs[head], own(ups[pair], e))
            query_t.append(dot(keys[pair][e * HD : (e + 1) * HD], made))
            if e == per - 1:
                grad_query = jnp.concatenate(query_t, axis=0).T
                for c, grad in enumerate((grad_query, grad_key, grad_value)):
                    grads[:, c * part + at : c * part + at + LANES] = grad.astype(BF)
        made = grads[...]
        sums[...] = jnp.sum(made.astype(F32), axis=0, keepdims=True)
        product = dot(made, tile[:, : 3 * part], NT)

        @pl.when(step == 0)
        def _():
            back[...] = product

        @pl.when(step > 0)
        def _():
            back[...] += product

    fixed = pl.BlockSpec((rows, width), lambda j: (0, 0))
    wide_rows = pl.BlockSpec((rows, 3 * part), lambda j: (0, j))
    return call(
        body,
        (halves,),
        [fixed]
        + specs
        + [
            wide_rows,
            pl.BlockSpec((heads, rows, rows), lambda j: (j, 0, 0)),
            pl.BlockSpec((1, heads, rows), lambda j: (j, 0, 0)),
        ],
        [
            (wide_rows, far_shape((rows, halves * 3 * part), BF)),
            (pl.BlockSpec((1, 3 * part), lambda j: (0, j)), shape((1, halves * 3 * part), F32)),
            (fixed, far_shape((rows, width), F32)),
        ],
        (Near(grad_low), *weights, qkv, probs, inverses),
        flops=2 * rows * width * total + halves * heads * 8 * rows * rows * HD,
        name="attend_back",
    )


def finish(inputs, middle, mlps, grad_middle, backs, keep, gain, down_bias, meta, places):
    rows, width = inputs.shape
    block = 128
    part = width // places
    count = len(mlps)

    def body(meta, x, middle, grad, keep, *refs):
        gain, bias, output, input_grad, sums = refs[2 * count :]
        mlp, upstream = refs[0][...], refs[count][...]
        for k in range(1, count):
            mlp = mlp + refs[k][...]
            upstream = upstream + refs[count + k][...]
        out = (middle[...] + mlp + columns(meta, bias, places, part)) * keep[...]
        normal, scaled = norm_stats(columns(meta, x, places, part).astype(F32))
        back = grad[...] + norm_back(upstream, columns(meta, gain, places, part), normal, scaled)

        @pl.when(pl.program_id(0) == 0)
        def _():
            sums[...] = jnp.zeros_like(sums)

        gains = jnp.sum(upstream * normal, axis=0, keepdims=True)
        shifts = jnp.sum(upstream, axis=0, keepdims=True)
        for r in range(places):
            spot = pl.ds(pl.multiple_of(meta[r], part), part)
            here = slice(r * part, (r + 1) * part)
            output[:, spot] = out[:, here].astype(BF)
            input_grad[:, spot] = back[:, here].astype(BF)
            sums[0:1, spot] += gains[:, here]
            sums[1:2, spot] += shifts[:, here]

    tall = pl.BlockSpec((block, width), lambda i, *_: (i, 0))
    vector = pl.BlockSpec((1, width), lambda i, *_: (0, 0))
    mark = pl.BlockSpec((block, 1), lambda i, *_: (i, 0))
    return call(
        body,
        (rows // block,),
        [tall, tall, tall, mark] + [tall] * (2 * count) + [vector, vector],
        [
            (tall, shape((rows, width), BF)),
            (tall, shape((rows, width), BF)),
            (pl.BlockSpec((2, width), lambda i, *_: (0, 0)), shape((2, width), F32)),
        ],
        (meta, inputs, middle, grad_middle, keep, *mlps, *backs, gain, down_bias),
        tables=1,
        name="finish",
    )


def bundle_plan(members, halves):
    plan = {"x": [(1, y, 0) for y in members]}
    for y in members:
        if y:
            plan["keep", y] = [(0, y, 0)]
            if halves > 1:
                plan["y", y] = [(0, y, 1), (1, y, 1)]
    if 0 in members:
        if halves > 1:
            plan["far"] = [(1, 0, 1)]
        plan["own"] = [(0, 0, h) for h in range(halves)]
    return plan


def urgent(name):
    return name == "x" or name[0] == "y"


def alone(name):
    return urgent(name) or name == "far"


def weight_grads(plan, lefts, rights, blocks, halves):
    width, rows = lefts[0].shape
    part = width // 4
    lines = len(rights)
    first = min(y for made in plan.values() for _, y, _ in made) * halves // blocks
    spans = [array.shape[1] // blocks for array in rights[0]]
    wide = sum(spans)
    kinds = len(spans)
    order = []
    for made in plan.values():
        order += [block[1:] for block in made if block[1:] not in order]
    names = list(plan)
    rest = [block for name in names if not alone(name) for block in plan[name]]
    outs, joint = [], {}
    for core in range(2):
        for name in names:
            steps = [order.index(block[1:]) for block in plan[name]]
            joint[name] = len(set(steps)) == 1
            size = wide * (len(steps) if joint[name] else 1)
            starts = [] if joint[name] else steps[1:]

            def index(i, starts=starts):
                at = 0
                for start in starts:
                    at = at + (i >= start).astype(jnp.int32)
                return (0, at)

            if not core or alone(name):
                outs.append(
                    (pl.BlockSpec((part, size), index), far_shape((part, wide * len(steps)), BF))
                )
    whole = (part, wide * len(rest))
    outs.append((pl.BlockSpec(whole, lambda i: (0, 0)), far_shape(whole, BF)))

    def body(*refs):
        left_refs = refs[:kinds]
        right_refs = [refs[kinds + g * kinds : kinds + (g + 1) * kinds] for g in range(lines)]
        out_refs = refs[kinds + lines * kinds :]
        step = pl.program_id(0)
        for s, (y, h) in enumerate(order):

            @pl.when(step == s)
            def _(y=y, h=h):
                line = (y * halves + h) // blocks - first
                for r in range(4):
                    x, core = divmod(r, 2)
                    here = slice(r * part, (r + 1) * part)
                    products = [
                        dot(left_refs[k][here, :], right_refs[line][k][...]).astype(BF)
                        for k in range(kinds)
                    ]
                    value = jnp.concatenate(products, axis=1) if kinds > 1 else products[0]
                    if core and (x, y, h) in rest:
                        at = rest.index((x, y, h)) * wide
                        out_refs[-1][:, at : at + wide] = value
                        continue
                    sent = [name for name in names if alone(name)]
                    for n, name in enumerate(sent if core else names):
                        if (x, y, h) in plan[name]:
                            at = plan[name].index((x, y, h)) * wide if joint[name] else 0
                            out_refs[core * len(names) + n][:, at : at + wide] = value

    def right_map(g):
        flat = [y * halves + h for y, h in order]
        mine = [(s, at % blocks) for s, at in enumerate(flat) if at // blocks - first == g]
        def index(i):
            at = mine[0][1]
            for (s0, h0), (s1, h1) in zip(mine, mine[1:]):
                at = at + jnp.where(i > s0, h1 - h0, 0)
            return (0, at)
        return index
    ins = [pl.BlockSpec((width, rows), lambda i: (0, 0)) for _ in lefts]
    operands = list(lefts)
    for g in range(lines):
        for k in range(kinds):
            ins.append(pl.BlockSpec((rows, spans[k]), right_map(g)))
            operands.append(rights[g][k])
    made = call(body, (len(order),), ins, outs, operands, name="weight_grads")
    mine = dict(zip(names, made[: len(names)]))
    sent = [name for name in names if alone(name)]
    return mine, dict(zip([*sent, "rest"], made[len(names) :])), rest


def all_weight_grads(left, rights, spots, groups, places, blocks):
    width, rows = left.shape
    part = width // places
    lines = len(rights)
    wide = rights[0].shape[1] // blocks
    count = lines * blocks
    per = count // groups

    def body(spots, left, *refs):
        right_refs, out = refs[:lines], refs[lines]
        step = pl.program_id(0)
        for line in range(lines):

            @pl.when((step >= line * blocks) & (step < (line + 1) * blocks))
            def _(line=line):
                for r in range(places):
                    here = left[r * part : (r + 1) * part, :]
                    out[0, spots[r]] = dot(here, right_refs[line][...]).astype(BF)

    def right(line):
        return pl.BlockSpec(
            (rows, wide), lambda i, *_: (0, jnp.clip(i - line * blocks, 0, blocks - 1))
        )

    def index(i, spots):
        return (spots[places + lax.div(i, jnp.int32(per))], 0, 0, lax.rem(i, jnp.int32(per)))

    return call(
        body,
        (count,),
        [pl.BlockSpec((width, rows), lambda i, *_: (0, 0))] + [right(k) for k in range(lines)],
        [
            (
                pl.BlockSpec((1, places, part, wide), index),
                far_shape((groups, places, part, wide * per), BF),
            )
        ],
        (spots, left, *rights),
        name="weight_grads",
        tables=1,
    )[0]


def shards(
    inputs,
    segments,
    first_gain,
    first_shift,
    qkv_weight,
    qv_bias,
    out_weight,
    out_bias,
    second_gain,
    second_shift,
    up_weight,
    up_bias,
    down_weight,
    down_bias,
    cotangent,
):
    groups = lax.axis_size("wide")
    copies = lax.axis_size("dp")
    places = lax.axis_size("narrow")
    place = lax.axis_index("narrow")
    member = lax.axis_index("wide")
    rows, width = inputs.shape
    part_width = qkv_weight.shape[2]
    hidden_width = up_weight.shape[1]
    part = width // places
    halves = 2 if part_width >= 2 * LANES else 1
    head_part = part_width // halves
    lines = min(2, groups)
    per_line = groups // lines
    steps = per_line * halves
    unit_steps = max(per_line, per_line * hidden_width // 512)

    def members(line):
        return range(line * per_line, (line + 1) * per_line)

    def swap(axis, mask):
        size = lax.axis_size(axis)
        pairs = [(i, i ^ mask) for i in range(size)]
        return lambda value: lax.ppermute(value, axis, pairs)

    core = swap("narrow", 1)
    over_x = swap("narrow", 2)
    over_y = [None] + [swap("wide", m) for m in range(1, groups)]

    spots = jnp.concatenate(
        [
            jnp.bitwise_xor(place, jnp.arange(places, dtype=jnp.int32)),
            jnp.bitwise_xor(member, jnp.arange(groups, dtype=jnp.int32)),
        ]
    )
    meta = spots[:places] * part
    row_of = lambda vector: vector.astype(F32).reshape(1, -1)
    keep = (segments >= 0).astype(F32).reshape(rows, 1)
    labels_col = segments.reshape(rows, 1)
    labels_row = segments.reshape(1, rows)

    three = qkv_weight.reshape(part, 3, halves, head_part)
    out_t = out_weight.T.reshape(part, 1, halves, head_part)
    packed = jnp.concatenate([three, out_t], axis=1).transpose(0, 2, 1, 3)
    packed = packed.reshape(part, 4 * part_width)
    small = jnp.concatenate([qv_bias.reshape(-1), up_bias]).reshape(1, -1)
    down_t = turned(down_weight, BF)

    def split(array):
        wide = array.shape[1] // halves
        return [array[:, h * wide : (h + 1) * wide] for h in range(halves)]

    def reach(own, *others):
        ready = after(own, *others) if others else own
        near = {(0, 0): [own], (1, 0): [over_x(ready)]}
        for y in range(1, groups):
            near[0, y] = [over_y[y](ready)]
        return near

    passed = []

    def forward_far(near):
        made = {}
        for y in range(1, groups):
            sent = [split(near[0, y][0])[0]]
            made[1, y] = [over_x(sent[0])]
            if halves > 1:
                sent.append(split(near[1, 0][0])[1])
                made[1, y].append(over_y[y](sent[1]))
            passed.extend(sent)
        return made

    def line_of(near, line):
        made = []
        for x in range(2):
            parts = [array for y in members(line) for array in near[x, y]]
            made.append(parts)
            made.append([core(array) for array in parts])
        return made

    small_all = [small] + [over_y[y](small) for y in range(1, groups)]

    turn = []

    def ordered(value, *others):
        return after(value, *turn, *others) if turn or others else value

    def done(made, key):
        turn[:] = [made[key]]
        return made

    def first_stage(near):
        return [near[1, 0][0]] + [near[0, y][0] for y in range(1, groups)]

    def held(near, *others):
        return {
            key: value if key == (0, 0) else [after(array, *others) for array in value]
            for key, value in near.items()
        }

    def all_of(weight):
        made = lax.all_gather(weight, ("wide", "narrow"), axis=0)
        return made.reshape(groups, places, *weight.shape)

    up_all = all_of(up_weight)
    attn_near = reach(packed)
    normed_one, normed_one_t, low, low_t = done(
        first_norm(
            inputs, cotangent, keep, row_of(first_gain), row_of(first_shift), meta, places
        ),
        0,
    )
    attn_near = held(attn_near, *turn)

    def qkv_bias(values):
        query = values[:, :part_width].reshape(halves, 1, head_part)
        value = values[:, part_width : 2 * part_width].reshape(halves, 1, head_part)
        return jnp.concatenate([query, jnp.zeros_like(query), value], axis=1).reshape(1, -1)

    forward = []
    attn_far = forward_far(attn_near)
    down_near = reach(down_t, *turn, *passed)
    first = {key: attn_far[key] for key in attn_far if key[1] < per_line}
    attn_pieces = [line_of(attn_near | first, 0)]
    for line in range(lines):
        if line:
            attn_near = held(attn_near | attn_far, *turn)
            attn_pieces.append(line_of(attn_near, line))
        bias = jnp.concatenate([qkv_bias(small_all[y]) for y in members(line)], axis=1)
        forward.append(
            done(
                attend(
                    ordered(normed_one, down_t), attn_pieces[line], bias, labels_col, labels_row, steps
                ),
                1,
            )
        )
    middle, normed_two, normed_two_t = done(
        second_norm(
            ordered(inputs),
            [f[4] for f in forward],
            row_of(out_bias),
            row_of(second_gain),
            row_of(second_shift),
            meta,
            places,
        ),
        0,
    )
    down_near = held(down_near, *turn)
    turn.extend(first_stage(down_near))
    down_far = forward_far(down_near)
    units = []
    for line in range(lines):
        bias = [small_all[y][:, 2 * part_width :] for y in members(line)]
        bias = jnp.concatenate(bias, axis=1)
        units.append(
            done(up(ordered(normed_two), up_all, bias, spots, line, lines, unit_steps), 0)
        )

    down_far = held(down_far, *turn)
    turn.extend(array for arrays in down_far.values() for array in arrays)
    block_width = 4 * head_part

    def cut(array, k):
        return array[:, k * block_width : (k + 1) * block_width].astype(F32)

    def grads_of(lefts, rights, ys=range(groups)):
        plan = bundle_plan(ys, halves)
        lefts = [ordered(lefts[0])] + lefts[1:]
        mine, other, rest = weight_grads(plan, lefts, rights, steps, halves)
        turn[:] = [next(iter(mine.values()))]
        came = {name: core(value) for name, value in other.items()}
        at = {}
        for name in mine:
            if not alone(name):
                at[name] = rest.index(plan[name][0]), len(plan[name])
        return ys, mine, came, at

    def both(made, name):
        _, mine, came, at = made
        if name in came:
            return mine[name].astype(F32) + ordered(came[name]).astype(F32)
        first, count = at[name]
        last = first + count
        came = ordered(came["rest"])[:, first * block_width : last * block_width]
        return mine[name].astype(F32) + came.astype(F32)

    def send_first(made):
        ys, mine = made[:2]
        sums = {name: both(made, name).astype(BF) for name in mine if urgent(name)}
        turn.extend(sums.values())
        got = {}
        for name, value in sums.items():
            if name == "x":
                from_x = over_x(value)
                got.update({("x", y): (from_x, k) for k, y in enumerate(ys)})
            else:
                got[name] = over_y[name[1]](value)
        return got

    def send_near(made, got, late):
        for y in made[0]:
            if y:
                array, k = got["x", y]
                value = (both(made, ("keep", y)) + cut(ordered(array), k)).astype(BF)
                turn.append(value)
                late[y] = over_y[y](value)

    def send_far(made, got, late):
        if halves > 1:
            value = both(made, "far")
            for y in range(1, groups):
                value = value + cut(ordered(got["y", y]), 1)
            value = value.astype(BF)
            turn.append(value)
            late["far"] = over_x(value)

    def total_of(parts, got, late):
        own = [both(made, "own") for made in parts if 0 in made[0]][0]
        late = {key: ordered(value).astype(F32) for key, value in late.items()}
        totals = [own[:, h * block_width : (h + 1) * block_width] for h in range(halves)]
        totals[0] = totals[0] + cut(*got["x", 0])
        for y in range(1, groups):
            totals[0] = totals[0] + late[y]
            if halves > 1:
                totals[1] = totals[1] + cut(got["y", y], 0)
        if halves > 1:
            totals[1] = totals[1] + late["far"]
        return totals

    copy_index = lax.axis_index("dp")
    masks = [1 << k for k in range(copies.bit_length() - 1)]
    bits = [(copy_index // mask) % 2 for mask in masks]

    def first_halve(totals):
        if len(totals) == 1:
            middle = block_width // 2
            totals = [totals[0][:, :middle], totals[0][:, middle:]]
        low, high = (t.astype(BF) for t in totals)
        away = jnp.where(bits[0] == 1, low, high)
        kept = jnp.where(bits[0] == 1, high, low)
        turn.extend([away, kept])
        return kept, swap("dp", masks[0])(away)

    def halve(state, k):
        kept, came = state
        value = kept.astype(F32) + ordered(came).astype(F32)
        half = value.shape[0] // 2
        away = lax.dynamic_slice_in_dim(value, (1 - bits[k]) * half, half, 0).astype(BF)
        kept = lax.dynamic_slice_in_dim(value, bits[k] * half, half, 0).astype(BF)
        turn.extend([away, kept])
        return kept, swap("dp", masks[k])(away)

    def join(state, k):
        kept, came = state
        came = ordered(came)
        if k == len(masks) - 1:
            value = (kept.astype(F32) + came.astype(F32)).astype(BF)
        else:
            value = jnp.where(
                bits[k + 1] == 1,
                jnp.concatenate([came, kept], axis=0),
                jnp.concatenate([kept, came], axis=0),
            )
        turn.extend([value])
        return value, swap("dp", masks[k])(value)

    def last_join(state, dtype=F32):
        value, came = state
        low = jnp.where(bits[0] == 1, came, value)
        high = jnp.where(bits[0] == 1, value, came)
        return jnp.concatenate([low, high], axis=1).astype(dtype)

    def vector_steps(vector):
        for axis, size in (("narrow", places), ("wide", groups), ("dp", copies)):
            mask = 1
            while mask < size:
                vector = vector + swap(axis, mask)(vector)
                yield vector
                mask *= 2

    first = {key: down_far[key] for key in down_far if key[1] < per_line}
    down_pieces = [line_of(down_near | first, 0)]
    down_grad = all_weight_grads(
        ordered(low_t), [u[0] for u in units], spots, groups, places, steps
    )
    turn[:] = [down_grad]
    down_pieces += [line_of(down_near | down_far, line) for line in range(1, lines)]
    down_grad = lax.psum_scatter(
        down_grad.reshape(groups * places, part, hidden_width),
        ("wide", "narrow"),
        scatter_dimension=0,
        tiled=True,
    )[0]
    back = []
    for line in range(lines):
        hidden, slope = units[line]
        back.append(
            done(
                mlp_back(
                    ordered(low),
                    hidden,
                    slope,
                    up_all,
                    down_pieces[line],
                    spots,
                    line,
                    lines,
                    unit_steps,
                ),
                0,
            )
        )
    up_made = grads_of([normed_two_t], [[b[0]] for b in back])
    grad_middle, grad_middle_low, grad_middle_t, second_sums = done(
        second_norm_back(
            ordered(middle), [b[3] for b in back], low, row_of(second_gain), meta, places
        ),
        0,
    )
    up_got = send_first(up_made)
    grads = [None] * lines

    def back_of(line):
        qkv, _, probs, inverses, _ = forward[line]
        grads[line] = done(
            attend_back(
                ordered(grad_middle_low), attn_pieces[line], qkv, probs, inverses, steps
            ),
            0,
        )

    attn_made, attn_got, attn_late, up_late = [], {}, {}, {}

    def attn_grads(line):
        rights = [[grads[line][0], forward[line][1]]]
        made = grads_of([normed_one_t, grad_middle_t], rights, members(line))
        attn_made.append(made)
        return made

    back_of(lines - 1)
    down_state = first_halve(
        [down_grad[:, : hidden_width // 2], down_grad[:, hidden_width // 2 :]]
    )
    for line in reversed(range(1, lines)):
        made = attn_grads(line)
        if line == lines - 1:
            send_near(up_made, up_got, up_late)
            send_far(up_made, up_got, up_late)
            for k in range(1, len(masks)):
                down_state = halve(down_state, k)
        back_of(line - 1)
        attn_got |= send_first(made)
    up_state = first_halve(total_of([up_made], up_got, up_late))
    output, input_grad, first_sums = done(
        finish(
            ordered(inputs),
            middle,
            [b[2] for b in back],
            grad_middle,
            [g[2] for g in grads],
            keep,
            row_of(first_gain),
            row_of(down_bias),
            meta,
            places,
        ),
        0,
    )
    def in_order(values):
        stacked = jnp.stack(values)
        index = jnp.bitwise_xor(member, jnp.arange(groups, dtype=jnp.int32))
        return jnp.take(stacked, index, axis=0)

    unit_sums = jnp.concatenate([b[1] for b in back], axis=1).reshape(groups, -1)
    unit_sums = in_order(list(unit_sums))
    head_sums = jnp.concatenate([g[1] for g in grads], axis=1)
    head_sums = in_order(list(head_sums.reshape(groups, halves, 3, head_part)))
    query_sums = head_sums[:, :, 0].reshape(-1)
    value_sums = head_sums[:, :, 2].reshape(-1)
    vector = jnp.concatenate(
        [
            second_sums.reshape(-1),
            first_sums.reshape(-1),
            unit_sums.reshape(-1),
            query_sums,
            value_sums,
        ]
    ).reshape(-1, LANES)
    for made in attn_made:
        send_near(made, attn_got, attn_late)
    for k in reversed(range(1, len(masks))):
        down_state = join(down_state, k)
    made = attn_grads(0)
    kernels = list(turn)
    attn_got |= send_first(made)
    send_near(made, attn_got, attn_late)
    send_far(made, attn_got, attn_late)
    last = list(turn)
    turn[:] = kernels
    down_state = join(down_state, 0)
    for k in range(1, len(masks)):
        up_state = halve(up_state, k)
    for k in reversed(range(len(masks))):
        up_state = join(up_state, k)
    turn[:] = last
    for vector in vector_steps(ordered(vector)):
        pass
    down_total = last_join(down_state, BF)
    state = first_halve(total_of(attn_made, attn_got, attn_late))
    for k in range(1, len(masks)):
        state = halve(state, k)
    for k in reversed(range(len(masks))):
        state = join(state, k)
    attn_total, up_total = last_join(state), last_join(up_state)
    vector = vector.reshape(-1)
    piece = lambda k: vector[k * width : (k + 1) * width]
    at = 6 * width
    units_all = hidden_width * groups
    line = member * places + place
    share = units_all // (groups * places)
    up_bias_grad = lax.dynamic_slice_in_dim(vector, at + line * share, share)
    at += units_all
    share = width // (groups * places)
    qv_bias_grad = jnp.stack(
        [
            lax.dynamic_slice_in_dim(vector, at + k * width + line * share, share)
            for k in range(2)
        ]
    )

    spans = [attn_total[:, k * head_part : (k + 1) * head_part] for k in range(4 * halves)]
    spans = [jnp.concatenate(spans[k::4], axis=1) for k in range(4)]
    qkv_grad = jnp.stack(spans[:3]).transpose(1, 0, 2)
    out_grad = turned(spans[3], F32)
    return (
        output,
        input_grad,
        piece(4),
        piece(5),
        qkv_grad,
        qv_bias_grad,
        out_grad,
        piece(2),
        piece(0),
        piece(1),
        up_total,
        up_bias_grad,
        turned(down_total, F32),
        piece(3),
    )


def solution(mesh):
    placed = (
        P(("dp", "wide", "narrow"), None),
        P(("dp", "wide", "narrow")),
        P(),
        P(),
        P("narrow", None, "wide"),
        P(None, "wide"),
        P("wide", "narrow"),
        P(),
        P(),
        P(),
        P("narrow", "wide"),
        P("wide"),
        P("wide", "narrow"),
        P(),
        P(("dp", "wide", "narrow"), None),
    )
    return jax.shard_map(
        shards,
        mesh=mesh,
        in_specs=placed,
        out_specs=(
            P(("dp", "wide", "narrow"), None),
            P(("dp", "wide", "narrow"), None),
            P(),
            P(),
            P("narrow", None, "wide"),
            P(None, ("wide", "narrow")),
            P("wide", "narrow"),
            P(),
            P(),
            P(),
            P("narrow", "wide"),
            P(("wide", "narrow")),
            P("wide", "narrow"),
            P(),
        ),
        check_vma=False,
    )
```

```python
from functools import partial

import jax
import jax.numpy as jnp
import numpy as np
from jax import lax
from jax.experimental import pallas as pl
from jax.experimental.pallas import tpu as pltpu
from jax.sharding import PartitionSpec as P

HD = 64
LEN = 512
LANES = 128
EPSILON = 1e-06
MASKED = -1e30
SQRT_HALF = 0.7071067811865476
DENSITY_SCALE = 0.3989422804014327
BF = jnp.bfloat16
F32 = jnp.float32
MIB = 1 << 20

COSTS = {
    "turned": 2,
    "first_norm": 5,
    "attend": 11,
    "second_norm": 5,
    "up": 6,
    "weight_grads": 10,
    "mlp_back": 13,
    "second_norm_back": 6,
    "attend_back": 14,
    "finish": 8,
}
COST_UNIT = 0.3 * 3.69e6

NN = (((1,), (0,)), ((), ()))
NT = (((1,), (1,)), ((), ()))


def dot(left, right, dims=NN):
    return lax.dot_general(left, right, dims, preferred_element_type=F32)


def call(body, grid, ins, outs, operands, scratch=(), flops=0, name=None, vmem=36, tables=0):
    operands = [
        o.value
        if isinstance(o, Near)
        else o
        if o.size * o.dtype.itemsize < MIB // 4
        else pltpu.with_memory_space_constraint(o, pltpu.HBM)
        for o in operands
    ]
    return pl.pallas_call(
        body,
        out_shape=[o for _, o in outs],
        grid_spec=pltpu.PrefetchScalarGridSpec(
            num_scalar_prefetch=tables,
            grid=grid,
            in_specs=ins,
            out_specs=[s for s, _ in outs],
            scratch_shapes=list(scratch),
        ),
        compiler_params=pltpu.CompilerParams(vmem_limit_bytes=vmem * MIB),
        cost_estimate=pl.CostEstimate(
            flops=0, bytes_accessed=int(COSTS[name] * COST_UNIT), transcendentals=0
        ),
        name=name,
    )(*operands)


def after(value, *others):
    return lax.optimization_barrier((value, *others))[0]


class Near:
    def __init__(self, value):
        self.value, self.shape, self.dtype = value, value.shape, value.dtype


def shape(dims, dtype):
    return jax.ShapeDtypeStruct(dims, dtype)


def far_shape(dims, dtype):
    return pltpu.HBM(dims, dtype)


def columns(meta, ref, places, width):
    return jnp.concatenate(
        [ref[:, pl.ds(pl.multiple_of(meta[r], width), width)] for r in range(places)], axis=1
    )


def norm_stats(values):
    average = jnp.mean(values, axis=-1, keepdims=True)
    centred = values - average
    variance = jnp.mean(centred * centred, axis=-1, keepdims=True)
    scaled = lax.rsqrt(variance + EPSILON)
    return centred * scaled, scaled


def norm_back(upstream, gain, normal, scaled):
    inner = upstream * gain
    first_term = jnp.mean(inner, axis=-1, keepdims=True)
    second_term = jnp.mean(inner * normal, axis=-1, keepdims=True)
    return scaled * (inner - first_term - normal * second_term)


def turned(array, dtype):
    rows, width = array.shape
    block = min(512, max(rows, width))

    def body(array, out):
        out[...] = array[...].astype(F32).T.astype(dtype)

    if rows > width:
        spec = pl.BlockSpec((block, width), lambda i: (i, 0))
        out = pl.BlockSpec((width, block), lambda i: (0, i))
    else:
        spec = pl.BlockSpec((rows, block), lambda i: (0, i))
        out = pl.BlockSpec((block, rows), lambda i: (i, 0))
    return call(
        body,
        (max(rows, width) // block,),
        [spec],
        [(out, far_shape((width, rows), dtype))],
        (array,),
        name="turned",
    )[0]


def first_norm(inputs, cotangent, keep, gain, shift, meta, places):
    rows, width = inputs.shape
    block = 128
    part = width // places

    def body(meta, x, cot, keep, gain, shift, normed, normed_t, low, low_t):
        normal, _ = norm_stats(columns(meta, x, places, part).astype(F32))
        out = normal * columns(meta, gain, places, part) + columns(meta, shift, places, part)
        normed[...] = out.astype(BF)
        normed_t[...] = out.T.astype(BF)
        grad = columns(meta, cot, places, part).astype(F32) * keep[...]
        low[...] = grad.astype(BF)
        low_t[...] = grad.T.astype(BF)

    tall = pl.BlockSpec((block, width), lambda i, *_: (i, 0))
    wide = pl.BlockSpec((width, block), lambda i, *_: (0, i))
    vector = pl.BlockSpec((1, width), lambda i, *_: (0, 0))
    mark = pl.BlockSpec((block, 1), lambda i, *_: (i, 0))
    return call(
        body,
        (rows // block,),
        [tall, tall, mark, vector, vector],
        [
            (tall, shape((rows, width), BF)),
            (wide, far_shape((width, rows), BF)),
            (tall, far_shape((rows, width), BF)),
            (wide, far_shape((width, rows), BF)),
        ],
        (meta, inputs, cotangent, keep, gain, shift),
        tables=1,
        name="first_norm",
    )


def tile_of(refs, step, steps):
    blocks = []
    for parts in refs:
        value = parts[0][...]
        for k in range(1, len(parts)):
            value = jnp.where(step >= k * (steps // len(parts)), parts[k][...], value)
        blocks.append(value)
    return jnp.concatenate(blocks, axis=0)


def tile_specs(pieces, width, steps):
    specs, operands, counts = [], [], []
    for parts in pieces:
        counts.append(len(parts))
        per = steps // len(parts)
        for k, array in enumerate(parts):
            specs.append(
                pl.BlockSpec(
                    (array.shape[0], width),
                    lambda j, *_, k=k, per=per: (0, jnp.clip(j - k * per, 0, per - 1)),
                )
            )
            operands.append(array)
    return specs, operands, counts


def regroup(refs, counts):
    grouped, at = [], 0
    for count in counts:
        grouped.append(refs[at : at + count])
        at += count
    return grouped


def attend(normed, pieces, bias, labels_col, labels_row, halves):
    rows, width = normed.shape
    total = sum(p.shape[1] for p in pieces[0])
    wide = total // halves
    part = wide // 4
    heads = part // HD
    specs, weights, counts = tile_specs(pieces, wide, halves)

    def body(normed, *refs):
        weight_refs = regroup(refs[: len(weights)], counts)
        bias, lc, lr, qkv, attended, probs, inverses, branch, mask = refs[len(weights) :]
        step = pl.program_id(0)

        @pl.when(step == 0)
        def _():
            mask[...] = jnp.where(lc[...] == lr[...], 0.0, MASKED)

        tile = tile_of(weight_refs, step, halves)
        projected = dot(normed[...], tile[:, : 3 * part]) + bias[...].astype(F32)
        low = projected.astype(BF)
        qkv[...] = low
        lane = lax.broadcasted_iota(jnp.int32, (1, LANES), 1)
        per = LANES // HD
        queries, keys, values = [], [], []
        for pair in range(part // LANES):
            at = pair * LANES
            queries.append(low[:, at : at + LANES] * jnp.asarray(HD**-0.5, BF))
            keys.append(low[:, part + at : part + at + LANES])
            values.append(low[:, 2 * part + at : 2 * part + at + LANES].T)

        def scores_of(head):
            pair, e = divmod(head, per)
            mine = (lane >= e * HD) & (lane < (e + 1) * HD)
            key = jnp.where(mine, keys[pair], jnp.zeros_like(keys[pair]))
            return dot(key, queries[pair], NT)

        coming, outs = scores_of(0), []
        for head in range(heads):
            scores = coming
            if head + 1 < heads:
                coming = scores_of(head + 1)
            pair, e = divmod(head, per)
            scores = scores + mask[...]
            weight = jnp.exp(scores - jnp.max(scores, axis=0, keepdims=True))
            inverse = 1.0 / jnp.sum(weight, axis=0, keepdims=True)
            prob = weight.astype(BF)
            probs[head] = prob
            inverses[0, head : head + 1, :] = inverse
            outs.append(dot(values[pair][e * HD : (e + 1) * HD], prob) * inverse)
            if e == per - 1:
                at = pair * LANES
                attended[:, at : at + LANES] = jnp.concatenate(outs, axis=0).T.astype(BF)
                outs = []
        product = dot(attended[...], tile[:, 3 * part :], NT)

        @pl.when(step == 0)
        def _():
            branch[...] = product

        @pl.when(step > 0)
        def _():
            branch[...] += product

    fixed = lambda *dims: pl.BlockSpec(dims, lambda j, *_: (0,) * len(dims))
    return call(
        body,
        (halves,),
        [fixed(rows, width)]
        + specs
        + [pl.BlockSpec((1, 3 * part), lambda j: (0, j)), fixed(rows, 1), fixed(1, rows)],
        [
            (pl.BlockSpec((rows, 3 * part), lambda j: (0, j)), far_shape((rows, halves * 3 * part), BF)),
            (pl.BlockSpec((rows, part), lambda j: (0, j)), far_shape((rows, halves * part), BF)),
            (
                pl.BlockSpec((heads, rows, rows), lambda j: (j, 0, 0)),
                far_shape((halves * heads, rows, rows), BF),
            ),
            (pl.BlockSpec((1, heads, rows), lambda j: (j, 0, 0)), shape((halves, heads, rows), F32)),
            (fixed(rows, width), shape((rows, width), F32)),
        ],
        (Near(normed), *weights, bias, labels_col, labels_row),
        scratch=[pltpu.VMEM((rows, rows), F32)],
        flops=2 * rows * width * total + halves * heads * 8 * rows * rows * HD,
        name="attend",
    )


def second_norm(inputs, branches, out_bias, gain, shift, meta, places):
    rows, width = inputs.shape
    block = 128
    part = width // places
    count = len(branches)

    def body(meta, x, *refs):
        bias, gain, shift, middle, normed, normed_t = refs[count:]
        value = columns(meta, x, places, part).astype(F32)
        total = refs[0][...]
        for ref in refs[1:count]:
            total = total + ref[...]
        value = value + total + columns(meta, bias, places, part)
        middle[...] = value
        normal, _ = norm_stats(value)
        out = normal * columns(meta, gain, places, part) + columns(meta, shift, places, part)
        normed[...] = out.astype(BF)
        normed_t[...] = out.T.astype(BF)

    tall = pl.BlockSpec((block, width), lambda i, *_: (i, 0))
    wide = pl.BlockSpec((width, block), lambda i, *_: (0, i))
    vector = pl.BlockSpec((1, width), lambda i, *_: (0, 0))
    return call(
        body,
        (rows // block,),
        [tall] * (1 + count) + [vector] * 3,
        [
            (tall, far_shape((rows, width), F32)),
            (tall, shape((rows, width), BF)),
            (wide, far_shape((width, rows), BF)),
        ],
        (meta, inputs, *map(Near, branches), out_bias, gain, shift),
        tables=1,
        name="second_norm",
    )


def tiles_of(gathered, groups, line, lines, steps):
    places, part, columns_all = gathered.shape[1:]
    per_line = groups // lines
    per = steps // per_line
    wide = columns_all // per

    def spec(r):
        def index(j, spots):
            y = line * per_line + lax.div(j, jnp.int32(per))
            return (spots[places + y], spots[r], 0, lax.rem(j, jnp.int32(per)))

        return pl.BlockSpec((1, 1, part, wide), index)

    return [spec(r) for r in range(places)], wide


def joined(refs):
    return jnp.concatenate([ref[0, 0] for ref in refs], axis=0)


def up(normed, gathered, bias, spots, line, lines, steps):
    rows, width = normed.shape
    groups, places = gathered.shape[:2]
    specs, wide = tiles_of(gathered, groups, line, lines, steps)
    total = wide * steps

    def body(spots, normed, *refs):
        bias, hidden, slope = refs[places:]
        before = dot(normed[...], joined(refs[:places])) + bias[...].astype(F32)
        below = 0.5 * (1.0 + lax.erf(before * SQRT_HALF))
        hidden[...] = (before * below).astype(BF)
        density = jnp.exp(before * before * -0.5) * DENSITY_SCALE
        slope[...] = (below + before * density).astype(BF)

    tall = pl.BlockSpec((rows, wide), lambda j, *_: (0, j))
    return call(
        body,
        (steps,),
        [pl.BlockSpec((rows, width), lambda j, *_: (0, 0))]
        + specs
        + [pl.BlockSpec((1, wide), lambda j, *_: (0, j))],
        [(tall, far_shape((rows, total), BF)), (tall, far_shape((rows, total), BF))],
        (spots, Near(normed), *[gathered] * places, bias),
        name="up",
        tables=1,
    )


def mlp_back(low, hidden, slope, up_all, down_pieces, spots, line, lines, steps):
    rows, width = low.shape
    groups, places = up_all.shape[:2]
    specs, wide = tiles_of(up_all, groups, line, lines, steps)
    total = wide * steps

    down_specs, down_weights, counts = tile_specs(down_pieces, wide, steps)
    count = len(down_weights)

    def body(spots, low, hidden, slope, *refs):
        before, sums, mlp, normed = refs[places + count :]
        step = pl.program_id(0)
        up_tile = joined(refs[:places])
        down_tile = tile_of(regroup(refs[places : places + count], counts), step, steps)
        grad = dot(low[...], down_tile) * slope[...].astype(F32)
        grad_low = grad.astype(BF)
        before[...] = grad_low
        sums[...] = jnp.sum(grad_low.astype(F32), axis=0, keepdims=True)
        product = dot(hidden[...], down_tile, NT)
        back = dot(grad_low, up_tile, NT)

        @pl.when(step == 0)
        def _():
            mlp[...] = product
            normed[...] = back

        @pl.when(step > 0)
        def _():
            mlp[...] += product
            normed[...] += back

    fixed = pl.BlockSpec((rows, width), lambda j, *_: (0, 0))
    tall = pl.BlockSpec((rows, wide), lambda j, *_: (0, j))
    return call(
        body,
        (steps,),
        [fixed, tall, tall] + specs + down_specs,
        [
            (tall, far_shape((rows, total), BF)),
            (pl.BlockSpec((1, wide), lambda j, *_: (0, j)), shape((1, total), F32)),
            (fixed, far_shape((rows, width), F32)),
            (fixed, shape((rows, width), F32)),
        ],
        (spots, low, hidden, slope, *[up_all] * places, *down_weights),
        name="mlp_back",
        tables=1,
    )


def second_norm_back(middle, backs, low, gain, meta, places):
    rows, width = middle.shape
    block = 128
    part = width // places
    count = len(backs)

    def body(meta, middle, low, *refs):
        gain, grad, grad_low, grad_t, sums = refs[count:]
        upstream = refs[0][...]
        for ref in refs[1:count]:
            upstream = upstream + ref[...]
        normal, scaled = norm_stats(middle[...])
        out = low[...].astype(F32)
        total = out + norm_back(upstream, columns(meta, gain, places, part), normal, scaled)
        grad[...] = total
        grad_low[...] = total.astype(BF)
        grad_t[...] = total.T.astype(BF)

        @pl.when(pl.program_id(0) == 0)
        def _():
            sums[...] = jnp.zeros_like(sums)

        for k, value in enumerate((upstream * normal, upstream, total, out)):
            added = jnp.sum(value, axis=0, keepdims=True)
            for r in range(places):
                spot = pl.ds(pl.multiple_of(meta[r], part), part)
                sums[k : k + 1, spot] += added[:, r * part : (r + 1) * part]

    tall = pl.BlockSpec((block, width), lambda i, *_: (i, 0))
    wide = pl.BlockSpec((width, block), lambda i, *_: (0, i))
    vector = pl.BlockSpec((1, width), lambda i, *_: (0, 0))
    return call(
        body,
        (rows // block,),
        [tall, tall] + [tall] * count + [vector],
        [
            (tall, far_shape((rows, width), F32)),
            (tall, shape((rows, width), BF)),
            (wide, far_shape((width, rows), BF)),
            (pl.BlockSpec((4, width), lambda i, *_: (0, 0)), shape((4, width), F32)),
        ],
        (meta, middle, low, *map(Near, backs), gain),
        tables=1,
        name="second_norm_back",
    )


def attend_back(grad_low, pieces, qkv, probs, inverses, halves):
    rows, width = grad_low.shape
    total = sum(p.shape[1] for p in pieces[0])
    wide = total // halves
    part = wide // 4
    heads = part // HD
    specs, weights, counts = tile_specs(pieces, wide, halves)

    def body(grad_low, *refs):
        weight_refs = regroup(refs[: len(weights)], counts)
        qkv, probs, inverses, grads, sums, back = refs[len(weights) :]
        step = pl.program_id(0)
        tile = tile_of(weight_refs, step, halves)
        upstream = dot(grad_low[...], tile[:, 3 * part :]).astype(BF)
        lane = lax.broadcasted_iota(jnp.int32, (1, LANES), 1)
        factor = HD**-0.5
        per = LANES // HD
        queries, keys, values, ups = [], [], [], []
        for pair in range(part // LANES):
            at = pair * LANES
            queries.append(qkv[:, at : at + LANES] * jnp.asarray(factor, BF))
            key = qkv[:, part + at : part + at + LANES]
            keys.append((key * jnp.asarray(factor, BF)).T)
            values.append(qkv[:, 2 * part + at : 2 * part + at + LANES])
            up_t = upstream[:, at : at + LANES].T.astype(F32)
            scaled = [
                up_t[e * HD : (e + 1) * HD] * inverses[0, pair * per + e : pair * per + e + 1, :]
                for e in range(per)
            ]
            ups.append(jnp.concatenate(scaled, axis=0).T.astype(BF))

        def own(value, e):
            mine = (lane >= e * HD) & (lane < (e + 1) * HD)
            return jnp.where(mine, value, jnp.zeros_like(value))

        def first_of(head):
            pair, e = divmod(head, per)
            return dot(own(values[pair], e), ups[pair], NT)

        coming = first_of(0)
        for head in range(heads):
            pair, e = divmod(head, per)
            at = pair * LANES
            grad_probs = coming
            if head + 1 < heads:
                coming = first_of(head + 1)
            prob = probs[head].astype(F32)
            delta = jnp.sum(prob * grad_probs, axis=0, keepdims=True)
            delta = delta * inverses[0, head : head + 1, :]
            made = (prob * (grad_probs - delta)).astype(BF)
            if e == 0:
                grad_key = dot(made, own(queries[pair], e))
                grad_value = dot(probs[head], own(ups[pair], e))
                query_t = []
            else:
                grad_key = grad_key + dot(made, own(queries[pair], e))
                grad_value = grad_value + dot(probs[head], own(ups[pair], e))
            query_t.append(dot(keys[pair][e * HD : (e + 1) * HD], made))
            if e == per - 1:
                grad_query = jnp.concatenate(query_t, axis=0).T
                for c, grad in enumerate((grad_query, grad_key, grad_value)):
                    grads[:, c * part + at : c * part + at + LANES] = grad.astype(BF)
        made = grads[...]
        sums[...] = jnp.sum(made.astype(F32), axis=0, keepdims=True)
        product = dot(made, tile[:, : 3 * part], NT)

        @pl.when(step == 0)
        def _():
            back[...] = product

        @pl.when(step > 0)
        def _():
            back[...] += product

    fixed = pl.BlockSpec((rows, width), lambda j: (0, 0))
    wide_rows = pl.BlockSpec((rows, 3 * part), lambda j: (0, j))
    return call(
        body,
        (halves,),
        [fixed]
        + specs
        + [
            wide_rows,
            pl.BlockSpec((heads, rows, rows), lambda j: (j, 0, 0)),
            pl.BlockSpec((1, heads, rows), lambda j: (j, 0, 0)),
        ],
        [
            (wide_rows, far_shape((rows, halves * 3 * part), BF)),
            (pl.BlockSpec((1, 3 * part), lambda j: (0, j)), shape((1, halves * 3 * part), F32)),
            (fixed, far_shape((rows, width), F32)),
        ],
        (Near(grad_low), *weights, qkv, probs, inverses),
        flops=2 * rows * width * total + halves * heads * 8 * rows * rows * HD,
        name="attend_back",
    )


def finish(inputs, middle, mlps, grad_middle, backs, keep, gain, down_bias, meta, places):
    rows, width = inputs.shape
    block = 128
    part = width // places
    count = len(mlps)

    def body(meta, x, middle, grad, keep, *refs):
        gain, bias, output, input_grad, sums = refs[2 * count :]
        mlp, upstream = refs[0][...], refs[count][...]
        for k in range(1, count):
            mlp = mlp + refs[k][...]
            upstream = upstream + refs[count + k][...]
        out = (middle[...] + mlp + columns(meta, bias, places, part)) * keep[...]
        normal, scaled = norm_stats(columns(meta, x, places, part).astype(F32))
        back = grad[...] + norm_back(upstream, columns(meta, gain, places, part), normal, scaled)

        @pl.when(pl.program_id(0) == 0)
        def _():
            sums[...] = jnp.zeros_like(sums)

        gains = jnp.sum(upstream * normal, axis=0, keepdims=True)
        shifts = jnp.sum(upstream, axis=0, keepdims=True)
        for r in range(places):
            spot = pl.ds(pl.multiple_of(meta[r], part), part)
            here = slice(r * part, (r + 1) * part)
            output[:, spot] = out[:, here].astype(BF)
            input_grad[:, spot] = back[:, here].astype(BF)
            sums[0:1, spot] += gains[:, here]
            sums[1:2, spot] += shifts[:, here]

    tall = pl.BlockSpec((block, width), lambda i, *_: (i, 0))
    vector = pl.BlockSpec((1, width), lambda i, *_: (0, 0))
    mark = pl.BlockSpec((block, 1), lambda i, *_: (i, 0))
    return call(
        body,
        (rows // block,),
        [tall, tall, tall, mark] + [tall] * (2 * count) + [vector, vector],
        [
            (tall, shape((rows, width), BF)),
            (tall, shape((rows, width), BF)),
            (pl.BlockSpec((2, width), lambda i, *_: (0, 0)), shape((2, width), F32)),
        ],
        (meta, inputs, middle, grad_middle, keep, *mlps, *backs, gain, down_bias),
        tables=1,
        name="finish",
    )


def bundle_plan(members, halves):
    plan = {"x": [(1, y, 0) for y in members]}
    for y in members:
        if y:
            plan["keep", y] = [(0, y, 0)]
            if halves > 1:
                plan["y", y] = [(0, y, 1), (1, y, 1)]
    if 0 in members:
        if halves > 1:
            plan["far"] = [(1, 0, 1)]
        plan["own"] = [(0, 0, h) for h in range(halves)]
    return plan


def urgent(name):
    return name == "x" or name[0] == "y"


def alone(name):
    return urgent(name) or name == "far"


def weight_grads(plan, lefts, rights, blocks, halves):
    width, rows = lefts[0].shape
    part = width // 4
    lines = len(rights)
    first = min(y for made in plan.values() for _, y, _ in made) * halves // blocks
    spans = [array.shape[1] // blocks for array in rights[0]]
    wide = sum(spans)
    kinds = len(spans)
    order = []
    for made in plan.values():
        order += [block[1:] for block in made if block[1:] not in order]
    names = list(plan)
    rest = [block for name in names if not alone(name) for block in plan[name]]
    outs, joint = [], {}
    for core in range(2):
        for name in names:
            steps = [order.index(block[1:]) for block in plan[name]]
            joint[name] = len(set(steps)) == 1
            size = wide * (len(steps) if joint[name] else 1)
            starts = [] if joint[name] else steps[1:]

            def index(i, starts=starts):
                at = 0
                for start in starts:
                    at = at + (i >= start).astype(jnp.int32)
                return (0, at)

            if not core or alone(name):
                outs.append(
                    (pl.BlockSpec((part, size), index), far_shape((part, wide * len(steps)), BF))
                )
    whole = (part, wide * len(rest))
    outs.append((pl.BlockSpec(whole, lambda i: (0, 0)), far_shape(whole, BF)))

    def body(*refs):
        left_refs = refs[:kinds]
        right_refs = [refs[kinds + g * kinds : kinds + (g + 1) * kinds] for g in range(lines)]
        out_refs = refs[kinds + lines * kinds :]
        step = pl.program_id(0)
        for s, (y, h) in enumerate(order):

            @pl.when(step == s)
            def _(y=y, h=h):
                line = (y * halves + h) // blocks - first
                for r in range(4):
                    x, core = divmod(r, 2)
                    here = slice(r * part, (r + 1) * part)
                    products = [
                        dot(left_refs[k][here, :], right_refs[line][k][...]).astype(BF)
                        for k in range(kinds)
                    ]
                    value = jnp.concatenate(products, axis=1) if kinds > 1 else products[0]
                    if core and (x, y, h) in rest:
                        at = rest.index((x, y, h)) * wide
                        out_refs[-1][:, at : at + wide] = value
                        continue
                    sent = [name for name in names if alone(name)]
                    for n, name in enumerate(sent if core else names):
                        if (x, y, h) in plan[name]:
                            at = plan[name].index((x, y, h)) * wide if joint[name] else 0
                            out_refs[core * len(names) + n][:, at : at + wide] = value

    def right_map(g):
        flat = [y * halves + h for y, h in order]
        mine = [(s, at % blocks) for s, at in enumerate(flat) if at // blocks - first == g]
        def index(i):
            at = mine[0][1]
            for (s0, h0), (s1, h1) in zip(mine, mine[1:]):
                at = at + jnp.where(i > s0, h1 - h0, 0)
            return (0, at)
        return index
    ins = [pl.BlockSpec((width, rows), lambda i: (0, 0)) for _ in lefts]
    operands = list(lefts)
    for g in range(lines):
        for k in range(kinds):
            ins.append(pl.BlockSpec((rows, spans[k]), right_map(g)))
            operands.append(rights[g][k])
    made = call(body, (len(order),), ins, outs, operands, name="weight_grads")
    mine = dict(zip(names, made[: len(names)]))
    sent = [name for name in names if alone(name)]
    return mine, dict(zip([*sent, "rest"], made[len(names) :])), rest


def all_weight_grads(left, rights, spots, groups, places, blocks):
    width, rows = left.shape
    part = width // places
    lines = len(rights)
    wide = rights[0].shape[1] // blocks
    count = lines * blocks
    per = count // groups

    def body(spots, left, *refs):
        right_refs, out = refs[:lines], refs[lines]
        step = pl.program_id(0)
        for line in range(lines):

            @pl.when((step >= line * blocks) & (step < (line + 1) * blocks))
            def _(line=line):
                for r in range(places):
                    here = left[r * part : (r + 1) * part, :]
                    out[0, spots[r]] = dot(here, right_refs[line][...]).astype(BF)

    def right(line):
        return pl.BlockSpec(
            (rows, wide), lambda i, *_: (0, jnp.clip(i - line * blocks, 0, blocks - 1))
        )

    def index(i, spots):
        return (spots[places + lax.div(i, jnp.int32(per))], 0, 0, lax.rem(i, jnp.int32(per)))

    return call(
        body,
        (count,),
        [pl.BlockSpec((width, rows), lambda i, *_: (0, 0))] + [right(k) for k in range(lines)],
        [
            (
                pl.BlockSpec((1, places, part, wide), index),
                far_shape((groups, places, part, wide * per), BF),
            )
        ],
        (spots, left, *rights),
        name="weight_grads",
        tables=1,
    )[0]


def shards(
    inputs,
    segments,
    first_gain,
    first_shift,
    qkv_weight,
    qv_bias,
    out_weight,
    out_bias,
    second_gain,
    second_shift,
    up_weight,
    up_bias,
    down_weight,
    down_bias,
    cotangent,
):
    groups = lax.axis_size("wide")
    copies = lax.axis_size("dp")
    places = lax.axis_size("narrow")
    place = lax.axis_index("narrow")
    member = lax.axis_index("wide")
    rows, width = inputs.shape
    part_width = qkv_weight.shape[2]
    hidden_width = up_weight.shape[1]
    part = width // places
    halves = 2 if part_width >= 2 * LANES else 1
    head_part = part_width // halves
    lines = min(2, groups)
    per_line = groups // lines
    steps = per_line * halves
    unit_steps = max(per_line, per_line * hidden_width // 512)

    def members(line):
        return range(line * per_line, (line + 1) * per_line)

    def swap(axis, mask):
        size = lax.axis_size(axis)
        pairs = [(i, i ^ mask) for i in range(size)]
        return lambda value: lax.ppermute(value, axis, pairs)

    core = swap("narrow", 1)
    over_x = swap("narrow", 2)
    over_y = [None] + [swap("wide", m) for m in range(1, groups)]

    spots = jnp.concatenate(
        [
            jnp.bitwise_xor(place, jnp.arange(places, dtype=jnp.int32)),
            jnp.bitwise_xor(member, jnp.arange(groups, dtype=jnp.int32)),
        ]
    )
    meta = spots[:places] * part
    row_of = lambda vector: vector.astype(F32).reshape(1, -1)
    keep = (segments >= 0).astype(F32).reshape(rows, 1)
    labels_col = segments.reshape(rows, 1)
    labels_row = segments.reshape(1, rows)

    three = qkv_weight.reshape(part, 3, halves, head_part)
    out_t = out_weight.T.reshape(part, 1, halves, head_part)
    packed = jnp.concatenate([three, out_t], axis=1).transpose(0, 2, 1, 3)
    packed = packed.reshape(part, 4 * part_width)
    small = jnp.concatenate([qv_bias.reshape(-1), up_bias]).reshape(1, -1)
    down_t = turned(down_weight, BF)

    def split(array):
        wide = array.shape[1] // halves
        return [array[:, h * wide : (h + 1) * wide] for h in range(halves)]

    def reach(own, *others):
        ready = after(own, *others) if others else own
        near = {(0, 0): [own], (1, 0): [over_x(ready)]}
        for y in range(1, groups):
            near[0, y] = [over_y[y](ready)]
        return near

    passed = []

    def forward_far(near):
        made = {}
        for y in range(1, groups):
            sent = [split(near[0, y][0])[0]]
            made[1, y] = [over_x(sent[0])]
            if halves > 1:
                sent.append(split(near[1, 0][0])[1])
                made[1, y].append(over_y[y](sent[1]))
            passed.extend(sent)
        return made

    def line_of(near, line):
        made = []
        for x in range(2):
            parts = [array for y in members(line) for array in near[x, y]]
            made.append(parts)
            made.append([core(array) for array in parts])
        return made

    small_all = [small] + [over_y[y](small) for y in range(1, groups)]

    turn = []

    def ordered(value, *others):
        return after(value, *turn, *others) if turn or others else value

    def done(made, key):
        turn[:] = [made[key]]
        return made

    def first_stage(near):
        return [near[1, 0][0]] + [near[0, y][0] for y in range(1, groups)]

    def held(near, *others):
        return {
            key: value if key == (0, 0) else [after(array, *others) for array in value]
            for key, value in near.items()
        }

    def all_of(weight):
        made = lax.all_gather(weight, ("wide", "narrow"), axis=0)
        return made.reshape(groups, places, *weight.shape)

    up_all = all_of(up_weight)
    attn_near = reach(packed)
    normed_one, normed_one_t, low, low_t = done(
        first_norm(
            inputs, cotangent, keep, row_of(first_gain), row_of(first_shift), meta, places
        ),
        0,
    )
    attn_near = held(attn_near, *turn, down_t, *small_all[1:])

    def qkv_bias(values):
        query = values[:, :part_width].reshape(halves, 1, head_part)
        value = values[:, part_width : 2 * part_width].reshape(halves, 1, head_part)
        return jnp.concatenate([query, jnp.zeros_like(query), value], axis=1).reshape(1, -1)

    forward = []
    attn_far = forward_far(attn_near)
    down_near = reach(down_t, *turn, *passed)
    first = {key: attn_far[key] for key in attn_far if key[1] < per_line}
    attn_pieces = [line_of(attn_near | first, 0)]
    for line in range(lines):
        if line:
            attn_near = held(attn_near | attn_far, *turn)
            attn_pieces.append(line_of(attn_near, line))
        bias = jnp.concatenate([qkv_bias(small_all[y]) for y in members(line)], axis=1)
        forward.append(
            done(
                attend(
                    ordered(normed_one, down_t), attn_pieces[line], bias, labels_col, labels_row, steps
                ),
                1,
            )
        )
    middle, normed_two, normed_two_t = done(
        second_norm(
            ordered(inputs),
            [f[4] for f in forward],
            row_of(out_bias),
            row_of(second_gain),
            row_of(second_shift),
            meta,
            places,
        ),
        0,
    )
    down_near = held(down_near, *turn)
    turn.extend(first_stage(down_near))
    down_far = forward_far(down_near)
    units = []
    for line in range(lines):
        bias = [small_all[y][:, 2 * part_width :] for y in members(line)]
        bias = jnp.concatenate(bias, axis=1)
        units.append(
            done(up(ordered(normed_two), up_all, bias, spots, line, lines, unit_steps), 0)
        )

    down_far = held(down_far, *turn)
    turn.extend(array for arrays in down_far.values() for array in arrays)
    block_width = 4 * head_part

    def cut(array, k):
        return array[:, k * block_width : (k + 1) * block_width].astype(F32)

    def grads_of(lefts, rights, ys=range(groups)):
        plan = bundle_plan(ys, halves)
        lefts = [ordered(lefts[0])] + lefts[1:]
        mine, other, rest = weight_grads(plan, lefts, rights, steps, halves)
        turn[:] = [next(iter(mine.values()))]
        came = {name: core(value) for name, value in other.items()}
        at = {}
        for name in mine:
            if not alone(name):
                at[name] = rest.index(plan[name][0]), len(plan[name])
        return ys, mine, came, at

    def both(made, name):
        _, mine, came, at = made
        if name in came:
            return mine[name].astype(F32) + ordered(came[name]).astype(F32)
        first, count = at[name]
        last = first + count
        came = ordered(came["rest"])[:, first * block_width : last * block_width]
        return mine[name].astype(F32) + came.astype(F32)

    def send_first(made):
        ys, mine = made[:2]
        sums = {name: both(made, name).astype(BF) for name in mine if urgent(name)}
        turn.extend(sums.values())
        got = {}
        for name, value in sums.items():
            if name == "x":
                from_x = over_x(value)
                got.update({("x", y): (from_x, k) for k, y in enumerate(ys)})
            else:
                got[name] = over_y[name[1]](value)
        return got

    def send_near(made, got, late):
        for y in made[0]:
            if y:
                array, k = got["x", y]
                value = (both(made, ("keep", y)) + cut(ordered(array), k)).astype(BF)
                turn.append(value)
                late[y] = over_y[y](value)

    def send_far(made, got, late):
        if halves > 1:
            value = both(made, "far")
            for y in range(1, groups):
                value = value + cut(ordered(got["y", y]), 1)
            value = value.astype(BF)
            turn.append(value)
            late["far"] = over_x(value)

    def total_of(parts, got, late):
        own = [both(made, "own") for made in parts if 0 in made[0]][0]
        late = {key: ordered(value).astype(F32) for key, value in late.items()}
        totals = [own[:, h * block_width : (h + 1) * block_width] for h in range(halves)]
        totals[0] = totals[0] + cut(*got["x", 0])
        for y in range(1, groups):
            totals[0] = totals[0] + late[y]
            if halves > 1:
                totals[1] = totals[1] + cut(got["y", y], 0)
        if halves > 1:
            totals[1] = totals[1] + late["far"]
        return totals

    copy_index = lax.axis_index("dp")
    masks = [1 << k for k in range(copies.bit_length() - 1)]
    bits = [(copy_index // mask) % 2 for mask in masks]

    def first_halve(totals):
        if len(totals) == 1:
            middle = block_width // 2
            totals = [totals[0][:, :middle], totals[0][:, middle:]]
        low, high = (t.astype(BF) for t in totals)
        away = jnp.where(bits[0] == 1, low, high)
        kept = jnp.where(bits[0] == 1, high, low)
        turn.extend([away, kept])
        return kept, swap("dp", masks[0])(away)

    def halve(state, k):
        kept, came = state
        value = kept.astype(F32) + ordered(came).astype(F32)
        half = value.shape[0] // 2
        away = lax.dynamic_slice_in_dim(value, (1 - bits[k]) * half, half, 0).astype(BF)
        kept = lax.dynamic_slice_in_dim(value, bits[k] * half, half, 0).astype(BF)
        turn.extend([away, kept])
        return kept, swap("dp", masks[k])(away)

    def join(state, k):
        kept, came = state
        came = ordered(came)
        if k == len(masks) - 1:
            value = (kept.astype(F32) + came.astype(F32)).astype(BF)
        else:
            value = jnp.where(
                bits[k + 1] == 1,
                jnp.concatenate([came, kept], axis=0),
                jnp.concatenate([kept, came], axis=0),
            )
        turn.extend([value])
        return value, swap("dp", masks[k])(value)

    def last_join(state, dtype=F32):
        value, came = state
        low = jnp.where(bits[0] == 1, came, value)
        high = jnp.where(bits[0] == 1, value, came)
        return jnp.concatenate([low, high], axis=1).astype(dtype)

    def vector_steps(vector):
        for axis, size in (("narrow", places), ("wide", groups), ("dp", copies)):
            mask = 1
            while mask < size:
                vector = vector + swap(axis, mask)(vector)
                yield vector
                mask *= 2

    first = {key: down_far[key] for key in down_far if key[1] < per_line}
    down_pieces = [line_of(down_near | first, 0)]
    down_grad = all_weight_grads(
        ordered(low_t), [u[0] for u in units], spots, groups, places, steps
    )
    turn[:] = [down_grad]
    down_pieces += [line_of(down_near | down_far, line) for line in range(1, lines)]
    down_grad = lax.psum_scatter(
        down_grad.reshape(groups * places, part, hidden_width),
        ("wide", "narrow"),
        scatter_dimension=0,
        tiled=True,
    )[0]
    back = []
    for line in range(lines):
        hidden, slope = units[line]
        back.append(
            done(
                mlp_back(
                    ordered(low),
                    hidden,
                    slope,
                    up_all,
                    down_pieces[line],
                    spots,
                    line,
                    lines,
                    unit_steps,
                ),
                0,
            )
        )
    up_made = grads_of([normed_two_t], [[b[0]] for b in back])
    grad_middle, grad_middle_low, grad_middle_t, second_sums = done(
        second_norm_back(
            ordered(middle), [b[3] for b in back], low, row_of(second_gain), meta, places
        ),
        0,
    )
    up_got = send_first(up_made)
    grads = [None] * lines

    def back_of(line):
        qkv, _, probs, inverses, _ = forward[line]
        grads[line] = done(
            attend_back(
                ordered(grad_middle_low), attn_pieces[line], qkv, probs, inverses, steps
            ),
            0,
        )

    attn_made, attn_got, attn_late, up_late = [], {}, {}, {}

    def attn_grads(line):
        rights = [[grads[line][0], forward[line][1]]]
        made = grads_of([normed_one_t, grad_middle_t], rights, members(line))
        attn_made.append(made)
        return made

    back_of(lines - 1)
    down_state = first_halve(
        [down_grad[:, : hidden_width // 2], down_grad[:, hidden_width // 2 :]]
    )
    for line in reversed(range(1, lines)):
        made = attn_grads(line)
        if line == lines - 1:
            send_near(up_made, up_got, up_late)
            send_far(up_made, up_got, up_late)
            for k in range(1, len(masks)):
                down_state = halve(down_state, k)
        back_of(line - 1)
        attn_got |= send_first(made)
    up_state = first_halve(total_of([up_made], up_got, up_late))
    output, input_grad, first_sums = done(
        finish(
            ordered(inputs),
            middle,
            [b[2] for b in back],
            grad_middle,
            [g[2] for g in grads],
            keep,
            row_of(first_gain),
            row_of(down_bias),
            meta,
            places,
        ),
        0,
    )
    def in_order(values):
        stacked = jnp.stack(values)
        index = jnp.bitwise_xor(member, jnp.arange(groups, dtype=jnp.int32))
        return jnp.take(stacked, index, axis=0)

    unit_sums = jnp.concatenate([b[1] for b in back], axis=1).reshape(groups, -1)
    unit_sums = in_order(list(unit_sums))
    head_sums = jnp.concatenate([g[1] for g in grads], axis=1)
    head_sums = in_order(list(head_sums.reshape(groups, halves, 3, head_part)))
    query_sums = head_sums[:, :, 0].reshape(-1)
    value_sums = head_sums[:, :, 2].reshape(-1)
    vector = jnp.concatenate(
        [
            second_sums.reshape(-1),
            first_sums.reshape(-1),
            unit_sums.reshape(-1),
            query_sums,
            value_sums,
        ]
    ).reshape(-1, LANES)
    for made in attn_made:
        send_near(made, attn_got, attn_late)
    for k in reversed(range(1, len(masks))):
        down_state = join(down_state, k)
    made = attn_grads(0)
    kernels = list(turn)
    attn_got |= send_first(made)
    send_near(made, attn_got, attn_late)
    send_far(made, attn_got, attn_late)
    last = list(turn)
    turn[:] = kernels
    down_state = join(down_state, 0)
    for k in range(1, len(masks)):
        up_state = halve(up_state, k)
    for k in reversed(range(len(masks))):
        up_state = join(up_state, k)
    turn[:] = last
    for vector in vector_steps(ordered(vector)):
        pass
    down_total = last_join(down_state, BF)
    state = first_halve(total_of(attn_made, attn_got, attn_late))
    for k in range(1, len(masks)):
        state = halve(state, k)
    for k in reversed(range(len(masks))):
        state = join(state, k)
    attn_total, up_total = last_join(state), last_join(up_state)
    vector = vector.reshape(-1)
    piece = lambda k: vector[k * width : (k + 1) * width]
    at = 6 * width
    units_all = hidden_width * groups
    line = member * places + place
    share = units_all // (groups * places)
    up_bias_grad = lax.dynamic_slice_in_dim(vector, at + line * share, share)
    at += units_all
    share = width // (groups * places)
    qv_bias_grad = jnp.stack(
        [
            lax.dynamic_slice_in_dim(vector, at + k * width + line * share, share)
            for k in range(2)
        ]
    )

    spans = [attn_total[:, k * head_part : (k + 1) * head_part] for k in range(4 * halves)]
    spans = [jnp.concatenate(spans[k::4], axis=1) for k in range(4)]
    qkv_grad = jnp.stack(spans[:3]).transpose(1, 0, 2)
    out_grad = turned(spans[3], F32)
    return (
        output,
        input_grad,
        piece(4),
        piece(5),
        qkv_grad,
        qv_bias_grad,
        out_grad,
        piece(2),
        piece(0),
        piece(1),
        up_total,
        up_bias_grad,
        turned(down_total, F32),
        piece(3),
    )


def solution(mesh):
    placed = (
        P(("dp", "wide", "narrow"), None),
        P(("dp", "wide", "narrow")),
        P(),
        P(),
        P("narrow", None, "wide"),
        P(None, "wide"),
        P("wide", "narrow"),
        P(),
        P(),
        P(),
        P("narrow", "wide"),
        P("wide"),
        P("wide", "narrow"),
        P(),
        P(("dp", "wide", "narrow"), None),
    )
    return jax.shard_map(
        shards,
        mesh=mesh,
        in_specs=placed,
        out_specs=(
            P(("dp", "wide", "narrow"), None),
            P(("dp", "wide", "narrow"), None),
            P(),
            P(),
            P("narrow", None, "wide"),
            P(None, ("wide", "narrow")),
            P("wide", "narrow"),
            P(),
            P(),
            P(),
            P("narrow", "wide"),
            P(("wide", "narrow")),
            P("wide", "narrow"),
            P(),
        ),
        check_vma=False,
    )
```
